128 devices in a mesh: outer: 8 (over z_hi, y), inner: 16 (over z_lo, x, core).
Axes of the slice: x: 4, y: 4, z: 4 (z_hi: 2, z_lo: 2; z = z_hi * 2 + z_lo), core: 2. Of those that a mesh axis runs over, the one named last changes fastest.
Arguments:
- queries: bfloat16 [32768, 2560], P(('outer', 'inner')), may hold values from -6 to 6
- keys: bfloat16 [32768, 2560], P(('outer', 'inner')), may hold values from -6 to 6
- values: bfloat16 [32768, 2560], P(('outer', 'inner')), may hold values from -6 to 6
- latents: bfloat16 [4096, 3, 2560], P(('outer', 'inner')), may hold values from -6 to 6
- latent_owner: int32 [1024], P(('outer', 'inner')), may hold values from 0 to 15, as said below
- token_source: int32 [32768], P(('outer', 'inner')), may hold values from -1 to 63, as said below
- doc_lengths: int32 [64], replicated, may hold values from 1 to 2048, 32768 in all
Outputs:
- attended: bfloat16 [32768, 2560], P(('outer', 'inner'))
The draws below stay inside these ranges and needn't reach their ends.
Inputs may be any that keep to these rules, and one draw needn't show every extreme that they name: `latent_owner`: the 8 images of one device go to distinct devices of its outer group, so at most 4 latent rows go from one device to one other; in every outer group some device receives an image from every device of the group. `token_source`: consistent with latent_owner: each image sent to a device fills 4 consecutive positions of that device's block, starting at a multiple of 4, in the order of its rows; every image fills exactly one such run.
All inputs are finite; a program needn't handle non-finite values.
Results may differ from the reference program's by a relative error of at most 0.004.
Values may be sent and summed in bfloat16 or wider, within the bound.
No kernel may reach another device: no remote copies, remote signals or barrier semaphores. Data moves between devices by JAX's collectives and lax.ppermute only.
A program may use at most 64 MiB of HBM per device.

```python
import math
import jax
import jax.numpy as jnp
import numpy as np
from jax import lax

HEADS = 20
HEAD = 128
LAT_IMG = 4
TOK_DEV = 256
IMG_DEV = 8
TOKENS = 32768
IMAGES = 1024
DOC_MAX = 2048
DOCS = 64
N_OUTER = 8
N_INNER = 16


def draw_queries(key, part):
    key = jax.random.fold_in(key, 11)
    base = jnp.clip(jax.random.normal(key, (TOKENS, HEADS * HEAD), jnp.float32), -6.0, 6.0)
    return base.astype(jnp.bfloat16)


def draw_keys(key, part):
    key = jax.random.fold_in(key, 12)
    base = jnp.clip(jax.random.normal(key, (TOKENS, HEADS * HEAD), jnp.float32), -6.0, 6.0)
    return base.astype(jnp.bfloat16)


def routing(key):
    inner_count = N_INNER
    groups = N_OUTER
    slots = TOK_DEV // LAT_IMG
    full = jax.random.randint(jax.random.fold_in(key, 201), (groups,), 0, inner_count)
    pair_keys = jax.random.split(jax.random.fold_in(key, 202), groups * inner_count)
    others = jax.vmap(lambda single: jax.random.permutation(single, inner_count - 1))(pair_keys)
    others = others[:, :IMG_DEV - 1].reshape(groups, inner_count, IMG_DEV - 1)
    full_spread = jnp.broadcast_to(full[:, None, None], (groups, inner_count, 1))
    others = others + (others >= full_spread).astype(jnp.int32)
    listed = jnp.concatenate([full_spread, others], axis=2)
    order_keys = jax.random.split(jax.random.fold_in(key, 203), groups * inner_count)
    order = jax.vmap(lambda single: jax.random.permutation(single, IMG_DEV))(order_keys).reshape(groups, inner_count, IMG_DEV)
    listed = jnp.take_along_axis(listed, order, axis=2)
    slot_keys = jax.random.split(jax.random.fold_in(key, 204), groups * inner_count)
    slot_of = jax.vmap(lambda single: jax.random.permutation(single, slots))(slot_keys)
    slot_of = slot_of[:, :inner_count].reshape(groups, inner_count, inner_count)
    owners = jnp.arange(inner_count, dtype=jnp.int32)
    sends = jnp.any(listed[:, :, :, None] == owners[None, None, None, :], axis=2)
    sends = jnp.transpose(sends, (0, 2, 1))
    place = jnp.arange(TOK_DEV, dtype=jnp.int32)
    match = (slot_of[:, :, None, :] == (place // LAT_IMG)[None, None, :, None]) & sends[:, :, None, :]
    label = owners[None, None, None, :] * LAT_IMG + (place % LAT_IMG)[None, None, :, None]
    source = jnp.sum(jnp.where(match, label, 0), axis=3) - 1 + jnp.any(match, axis=3).astype(jnp.int32)
    return (listed.reshape(-1).astype(jnp.int32), source.reshape(-1).astype(jnp.int32))


def draw_latent_owner(key, part):
    listed, source = routing(key)
    return listed


def draw_token_source(key, part):
    listed, source = routing(key)
    return source


def level_of(key, shape, cuts, least, high):
    def one(position, shards_of):
        heights = jax.random.uniform(jax.random.fold_in(jax.random.fold_in(key, 6), position), (shards_of,), jnp.float32, least / len(cuts), high / len(cuts))
        return jnp.repeat(jnp.exp(heights), shape[position] // shards_of).reshape((-1,) + (1,) * (len(shape) - position - 1))

    level = one(*cuts[0])
    for cut in cuts[1:]:
        level = level * one(*cut)
    return level


def length_profile(number_of, total, limit, skew):
    weights = [(1 << 20) // math.isqrt(standing ** skew) + 1 for standing in range(2, number_of + 1)]
    spare, holding = total - limit - (number_of - 1), [1] * (number_of - 1)
    while spare > 0:
        candidates = [i for i in range(number_of - 1) if holding[i] < limit]
        mass, budget = sum([weights[i] for i in candidates]), spare
        for i in candidates:
            extra = min(limit - holding[i], max(1, budget * weights[i] // mass), spare)
            holding[i] = holding[i] + extra
            spare = spare - extra
    return np.array([limit] + holding)


def ragged(own_key, amount, total, bound, skew):
    if amount == 2:
        one = jax.random.randint(own_key, (), max(1, total - bound), min(bound, total - 1) + 1)
        return jnp.stack([one, total - one])
    lengths = jnp.asarray(length_profile(amount, total, bound, skew), jnp.int32)
    couples = (amount - 1) // 2
    source_of, sink = lengths[1:1 + 2 * couples:2], lengths[2:2 + 2 * couples:2]
    room = jnp.minimum(source_of - 1, bound - sink)
    shifted = jax.random.randint(jax.random.fold_in(own_key, 1), (couples,), 0, 1 << 20) % (room + 1)
    lengths = lengths.at[1:1 + 2 * couples:2].set(source_of - shifted).at[2:2 + 2 * couples:2].set(sink + shifted)
    return lengths[jax.random.permutation(jax.random.fold_in(own_key, 2), amount)]


def noise(stream_key, extent, spread, most, pieces=(), kind=jnp.bfloat16):
    array = jax.random.normal(stream_key, extent, jnp.float32) * spread
    if len(pieces) > 0:
        array = level_of(stream_key, extent, pieces, -0.22, 0.18) * array
    return jnp.clip(array, min=-most, max=most).astype(kind)


def setup_inputs(seed: int = 0) -> dict:
    seeds = jax.random.split(jax.random.key(seed), 8)
    queries = draw_queries(jax.random.fold_in(seeds[7], 71), 0)
    keys = draw_keys(jax.random.fold_in(seeds[7], 71), 0)
    values = noise(seeds[2], (TOKENS, HEADS * HEAD), 1.0, 6.0, ((0, 128),))
    latents = noise(seeds[3], (IMAGES * LAT_IMG, 3, HEADS * HEAD), 1.0, 6.0, ((0, 128),))
    latent_owner = draw_latent_owner(jax.random.fold_in(seeds[7], 71), 0)
    token_source = draw_token_source(jax.random.fold_in(seeds[7], 71), 0)
    doc_lengths = ragged(seeds[6], DOCS, TOKENS, DOC_MAX, 2).astype(jnp.int32)
    return {"queries": queries, "keys": keys, "values": values, "latents": latents, "latent_owner": latent_owner, "token_source": token_source, "doc_lengths": doc_lengths}


masked_score = -1.0e30


def doc_starts(positions, doc_lengths):
    ends = jnp.cumsum(doc_lengths)
    begins = ends - doc_lengths
    inside = begins[None, :] <= positions[:, None]
    return jnp.max(jnp.where(inside, begins[None, :], 0), axis=1).astype(jnp.int32)


def reference(queries, keys, values, latents, latent_owner, token_source, doc_lengths):
    devices = N_OUTER * N_INNER
    width = HEADS * HEAD
    positions = jnp.arange(TOKENS, dtype=jnp.int32)
    block_of = positions // TOK_DEV
    group_of = block_of // N_INNER
    owner_inner = block_of % N_INNER
    chosen = jnp.maximum(token_source, 0)
    sender = group_of * N_INNER + chosen // LAT_IMG
    owned = latent_owner.reshape(devices, IMG_DEV)
    sender_owners = jnp.take(owned, sender, axis=0)
    match = sender_owners == owner_inner[:, None]
    image = jnp.sum(jnp.where(match, jnp.arange(IMG_DEV, dtype=jnp.int32)[None, :], 0), axis=1)
    latent_row = (sender * IMG_DEV + image) * LAT_IMG + chosen % LAT_IMG
    placed = jnp.take(latents, latent_row.astype(jnp.int32), axis=0)
    live = (token_source >= 0)[:, None]
    query_all = jnp.where(live, placed[:, 0], queries)
    key_all = jnp.where(live, placed[:, 1], keys)
    value_all = jnp.where(live, placed[:, 2], values)
    starts = doc_starts(positions, doc_lengths)
    reach = (N_INNER // 2) * TOK_DEV
    span = reach + TOK_DEV
    key_padded = jnp.concatenate([jnp.zeros((reach, width), jnp.bfloat16), key_all], axis=0)
    value_padded = jnp.concatenate([jnp.zeros((reach, width), jnp.bfloat16), value_all], axis=0)

    def one_block(index):
        first = (index * TOK_DEV).astype(jnp.int32)
        query_block = lax.dynamic_slice_in_dim(query_all, first, TOK_DEV, 0).astype(jnp.float32).reshape(TOK_DEV, HEADS, HEAD)
        key_block = lax.dynamic_slice_in_dim(key_padded, first, span, 0).astype(jnp.float32).reshape(span, HEADS, HEAD)
        value_block = lax.dynamic_slice_in_dim(value_padded, first, span, 0).astype(jnp.float32).reshape(span, HEADS, HEAD)
        query_pos = first + jnp.arange(TOK_DEV, dtype=jnp.int32)
        key_pos = first - reach + jnp.arange(span, dtype=jnp.int32)
        query_first = lax.dynamic_slice_in_dim(starts, first, TOK_DEV, 0)
        visible = (key_pos[None, :] <= query_pos[:, None]) & (key_pos[None, :] >= query_first[:, None])
        scores = jnp.einsum("thd,shd->hts", query_block, key_block) * (HEAD ** -0.5)
        scores = jnp.where(visible[None], scores, masked_score)
        top = jnp.max(scores, axis=2)
        weights = jnp.where(visible[None], jnp.exp(scores - top[:, :, None]), 0.0)
        total = jnp.sum(weights, axis=2)
        rounded = lax.optimization_barrier(weights.astype(jnp.bfloat16)).astype(jnp.float32)
        mixed = jnp.einsum("hts,shd->thd", rounded, value_block) / total.T[:, :, None]
        return mixed.reshape(TOK_DEV, width).astype(jnp.bfloat16)

    blocks = lax.map(one_block, jnp.arange(devices, dtype=jnp.int32))
    return blocks.reshape(TOKENS, width)
```

```python
import functools

import jax
import jax.numpy as jnp
from jax import lax
from jax.experimental import pallas as pl
from jax.experimental.pallas import tpu as pltpu
from jax.sharding import PartitionSpec as P

HEADS = 20
HEAD = 128
ROWS = 256
XS = 4
GROUP = HEADS // XS
WIDTH = GROUP * HEAD
BLOCKS = 8
AXES = ("outer", "inner")
CHUNKS = ((0, 1), (1, 2), (3, 2))
UNROLL = 4
SLOTS = 4 + 4 * 8 + 8

SCALE = HEAD ** (-0.5) * 1.4426950408889634
HIDDEN = -1e30
VMEM_LIMIT = 48 * 1024 * 1024


def routes(target):
    out = []
    for outer in range(8):
        for inner in range(16):
            to = target(outer * 16 + inner)
            if 0 <= to < 128:
                out.append((outer * 16 + inner, to))
    return out


def along_x(steps):
    return routes(lambda d: (d & ~7) | ((d + 2 * steps) & 7))


TO_CORE = routes(lambda d: d ^ 1)
TO_Z = routes(lambda d: d ^ 8)
TO_NEXT = routes(lambda d: d + 8)


def send(value, route):
    return lax.ppermute(value, AXES, route)


def across_x(parts):
    return [parts[0]] + [send(parts[XS - rel], along_x(XS - rel)) for rel in range(1, XS)]


def params():
    return pltpu.CompilerParams(vmem_limit_bytes=VMEM_LIMIT)


ANY = pl.BlockSpec(memory_space=pl.ANY)
SMEM = pl.BlockSpec(memory_space=pltpu.SMEM)
VMEM = pl.BlockSpec(memory_space=pltpu.VMEM)


def run_copies(copies, sems):
    started = [pltpu.make_async_copy(a, b, sems.at[n]) for n, (a, b) in enumerate(copies)]
    for copy in started:
        copy.start()
    for copy in started:
        copy.wait()


def pack_kernel(count, chunks, place, *refs):
    tensors, outs, sems = refs[:count], refs[count:-1], refs[-1]
    copies = []
    for rel in range(XS):
        column = ((place[0] + rel) & 3) * WIDTH
        for n, (first, heads) in enumerate(chunks):
            begin = pl.multiple_of(column + first * HEAD, HEAD)
            for t in range(count):
                copies.append((tensors[t].at[:, pl.ds(begin, heads * HEAD)], outs[n * XS + rel].at[t]))
    run_copies(copies, sems)


def pack(place, tensors, chunks):
    count = len(tensors)
    shapes = [
        jax.ShapeDtypeStruct((count, ROWS, heads * HEAD), jnp.bfloat16)
        for _, heads in chunks
        for _ in range(XS)
    ]
    outs = pl.pallas_call(
        functools.partial(pack_kernel, count, chunks),
        out_shape=shapes,
        in_specs=[SMEM] + [ANY] * count,
        out_specs=[ANY] * len(shapes),
        scratch_shapes=[pltpu.SemaphoreType.DMA((len(shapes) * count,))],
        compiler_params=params(),
    )(place, *tensors)
    return [outs[n * XS : (n + 1) * XS] for n in range(len(chunks))]


def pack_latents_kernel(slots, place, kinds, notes, *refs):
    outs, sems = refs[:-1], refs[-1]
    copies = []
    for rel in range(XS):
        column = ((place[0] + rel) & 3) * WIDTH
        for n, group in enumerate(slots):
            for s, slot in enumerate(group):
                if slot is None:
                    source = notes
                else:
                    kind, head = slot
                    source = kinds.at[kind, :, pl.ds(pl.multiple_of(column + head * HEAD, HEAD), HEAD)]
                copies.append((source, outs[n * XS + rel].at[s]))
    run_copies(copies, sems)


def pack_latents(place, kinds, notes, slots):
    rows = kinds.shape[1]
    shapes = [jax.ShapeDtypeStruct((len(group), rows, HEAD), jnp.bfloat16) for group in slots for _ in range(XS)]
    outs = pl.pallas_call(
        functools.partial(pack_latents_kernel, slots),
        out_shape=shapes,
        in_specs=[SMEM, ANY, ANY],
        out_specs=[ANY] * len(shapes),
        scratch_shapes=[pltpu.SemaphoreType.DMA((XS * sum(len(group) for group in slots),))],
        compiler_params=params(),
    )(place, kinds, notes)
    return [outs[n * XS : (n + 1) * XS] for n in range(len(slots))]


def merge_kernel(heads, kinds, slots, *refs):
    parts, (near, far, hot, keep, out, raw, lat, sems) = refs[:XS], refs[XS:]
    copies = [(near, lat.at[0]), (far, lat.at[1])] + [(parts[rel], raw.at[rel]) for rel in range(XS)]
    run_copies(copies, sems)
    work = [(t, h) for h in range(heads) for t in range(len(kinds))]
    for n in range(0, len(work), 2):
        pair = work[n : n + 2]
        columns = []
        for t, h in pair:
            rows = [lat[cc, zz, r, slots[h][t]] for cc in range(2) for zz in range(2) for r in range(XS)]
            columns.append(jnp.concatenate(rows, axis=0))
        columns = jnp.concatenate(columns, axis=1)
        for rel in range(XS):
            kept = keep[rel] > 0
            placed = jnp.dot(hot[rel], columns, preferred_element_type=jnp.float32)
            for p, (t, h) in enumerate(pair):
                lanes = slice(h * HEAD, (h + 1) * HEAD)
                merged = jnp.where(
                    kept, raw[rel, t, :, lanes].astype(jnp.float32), placed[:, p * HEAD : (p + 1) * HEAD]
                )
                if kinds[t] == 2:
                    merged = jnp.concatenate([merged[:HEAD].T, merged[HEAD:].T], axis=0)
                out[rel, t, :, lanes] = merged.astype(jnp.bfloat16)


def merge(parts, near, far, hot, keep, heads, kinds, slots):
    return pl.pallas_call(
        functools.partial(merge_kernel, heads, kinds, slots),
        out_shape=jax.ShapeDtypeStruct((XS, len(kinds), ROWS, heads * HEAD), jnp.bfloat16),
        in_specs=[ANY] * (XS + 2) + [VMEM] * 2,
        out_specs=VMEM,
        scratch_shapes=[
            pltpu.VMEM((XS, len(kinds), ROWS, heads * HEAD), jnp.bfloat16),
            pltpu.VMEM((2,) + near.shape, jnp.bfloat16),
            pltpu.SemaphoreType.DMA((XS + 2,)),
        ],
        compiler_params=params(),
    )(*parts, near, far, hot, keep)


def attend_kernel(first, heads, place, reach, begins, q_hbm, own, twin, own_before, twin_before, *refs):
    outs, (q_buf, kv_buf, scores, best, total, accum, item_q, item_j, sems) = refs[:XS], refs[XS:]
    x, core = place[0], place[1]
    copies = [(q_hbm.at[:, 0, :, pl.ds(first * HEAD, heads * HEAD)], q_buf)]
    for rel in range(XS):
        at = 2 * ((x + rel) & 3)
        copies.append((own.at[rel], kv_buf.at[BLOCKS + at + core]))
        copies.append((twin.at[rel], kv_buf.at[BLOCKS + at + 1 - core]))
        copies.append((own_before.at[rel], kv_buf.at[at + core]))
        copies.append((twin_before.at[rel], kv_buf.at[at + 1 - core]))
    started = [pltpu.make_async_copy(a, b, sems.at[n]) for n, (a, b) in enumerate(copies)]
    for copy in started:
        copy.start()

    mine = [BLOCKS + 2 * ((x + rel) & 3) + core for rel in range(XS)]

    def listed(count, low, high):
        for rel in range(XS):
            begin = low(rel)

            def add(j, count, rel=rel):
                item_q[count] = rel
                item_j[count] = j
                return count + 1

            count = lax.fori_loop(begin, high(rel), add, count)
        for extra in range(UNROLL - 1):
            item_q[count + extra] = XS
            item_j[count + extra] = BLOCKS
        return (count + UNROLL - 1) // UNROLL * UNROLL

    for rel in range(XS):
        item_q[rel] = rel
        item_j[rel] = mine[rel]
    edge = listed(XS, lambda rel: reach[rel, 0], lambda rel: reach[rel, 1])
    end = listed(edge, lambda rel: reach[rel, 1], lambda rel: mine[rel])

    for copy in started:
        copy.wait()

    key_row = lax.broadcasted_iota(jnp.int32, (ROWS, ROWS), 0)
    query_column = lax.broadcasted_iota(jnp.int32, (ROWS, ROWS), 1)

    for h in range(heads):
        lanes = slice(h * HEAD, (h + 1) * HEAD)
        best[...] = jnp.full(best.shape, HIDDEN, jnp.float32)
        total[...] = jnp.zeros(total.shape, jnp.float32)
        accum[...] = jnp.zeros(accum.shape, jnp.float32)

        def score(slot, edge, diagonal):
            q, j = item_q[slot], item_j[slot]
            tile = lax.dot_general(
                kv_buf[j, 0, :, lanes],
                q_buf[q & 3, :, lanes],
                (((1,), (1,)), ((), ())),
                preferred_element_type=jnp.float32,
            )
            if edge:
                seen = key_row >= begins[q & 3] - j * ROWS
                if diagonal:
                    seen = seen & (key_row <= query_column)
                tile = jnp.where(seen, tile, HIDDEN)
            scores[slot] = tile
            best[q] = jnp.maximum(best[q], jnp.max(tile.reshape(ROWS // 8, 8, ROWS), axis=0))

        def weigh(slot):
            q, j = item_q[slot], item_j[slot]
            weights = jnp.exp2(scores[slot] * SCALE - best[q, 0:1])
            total[q] = total[q] + jnp.sum(weights.reshape(ROWS // 8, 8, ROWS), axis=0)
            value = jnp.concatenate([kv_buf[j, 1, :HEAD, lanes], kv_buf[j, 1, HEAD:, lanes]], axis=1)
            accum[q] = accum[q] + jnp.dot(value, weights.astype(jnp.bfloat16), preferred_element_type=jnp.float32)

        def grouped(low, high, one):
            def several(n, carry):
                for extra in range(UNROLL):
                    one(n * UNROLL + extra)
                return carry

            lax.fori_loop(low // UNROLL, high // UNROLL, several, 0)

        for rel in range(XS):
            score(rel, True, True)
        grouped(XS, edge, lambda slot: score(slot, True, False))
        grouped(edge, end, lambda slot: score(slot, False, False))
        for q in range(XS + 1):
            best[q] = jnp.broadcast_to(jnp.max(best[q], axis=0, keepdims=True) * SCALE, (8, ROWS))
        grouped(0, end, weigh)
        for rel in range(XS):
            mixed = accum[rel] / jnp.sum(total[rel], axis=0, keepdims=True)
            outs[rel][:, lanes] = mixed.T.astype(jnp.bfloat16)


def attend(place, reach, begins, query, own, twin, own_before, twin_before, chunk):
    first, heads = chunk
    return pl.pallas_call(
        functools.partial(attend_kernel, first, heads),
        out_shape=[jax.ShapeDtypeStruct((ROWS, heads * HEAD), jnp.bfloat16)] * XS,
        in_specs=[SMEM, SMEM, VMEM] + [ANY] * 5,
        out_specs=[VMEM] * XS,
        scratch_shapes=[
            pltpu.VMEM((XS, ROWS, heads * HEAD), jnp.bfloat16),
            pltpu.VMEM((2 * BLOCKS, 2, ROWS, heads * HEAD), jnp.bfloat16),
            pltpu.VMEM((SLOTS, ROWS, ROWS), jnp.float32),
            pltpu.VMEM((XS + 1, 8, ROWS), jnp.float32),
            pltpu.VMEM((XS + 1, 8, ROWS), jnp.float32),
            pltpu.VMEM((XS + 1, HEAD, ROWS), jnp.float32),
            pltpu.SMEM((SLOTS + UNROLL,), jnp.int32),
            pltpu.SMEM((SLOTS + UNROLL,), jnp.int32),
            pltpu.SemaphoreType.DMA((4 * XS + 1,)),
        ],
        compiler_params=params(),
    )(place, reach, begins, query, own, twin, own_before, twin_before)


def unpack_kernel(chunks, place, *refs):
    parts, out, sems = refs[:-2], refs[-2], refs[-1]
    copies = []
    for n, (first, heads) in enumerate(chunks):
        for rel in range(XS):
            begin = pl.multiple_of(((place[0] + rel) & 3) * WIDTH + first * HEAD, HEAD)
            copies.append((parts[n * XS + rel], out.at[:, pl.ds(begin, heads * HEAD)]))
    run_copies(copies, sems)


def unpack(place, parts, chunks):
    return pl.pallas_call(
        functools.partial(unpack_kernel, chunks),
        out_shape=jax.ShapeDtypeStruct((ROWS, HEADS * HEAD), jnp.bfloat16),
        in_specs=[SMEM] + [ANY] * len(parts),
        out_specs=ANY,
        scratch_shapes=[pltpu.SemaphoreType.DMA((len(parts),))],
        compiler_params=params(),
    )(place, *parts)


def gathered(parts):
    near = jnp.stack(across_x(parts))
    near = jnp.stack([near, send(near, TO_Z)])
    return near, send(near, TO_CORE)


def per_device(queries, keys, values, latents, latent_owner, token_source, doc_lengths):
    outer = lax.axis_index("outer").astype(jnp.int32)
    inner = lax.axis_index("inner").astype(jnp.int32)
    z, x, core = inner >> 3, (inner >> 1) & 3, inner & 1
    place = jnp.stack([x, core])
    images = latent_owner.shape[0]

    notes = jnp.concatenate(
        [token_source, jnp.pad(latent_owner, (0, 32 * HEAD - ROWS - images))]
    ).reshape(32, HEAD).astype(jnp.bfloat16)
    slots = [[(kind, first + h) for h in range(heads) for kind in (1, 2)] for first, heads in CHUNKS]
    slots = [[None] + slots[0], sum(slots[1:], []) + [(0, h) for h in range(GROUP)]]
    packed_latents = pack_latents(place, latents.transpose(1, 0, 2), notes, slots)
    lat = [gathered(parts) for parts in packed_latents]

    def slot_of(first, heads, kinds):
        n = 0 if (kinds[0], first) in slots[0] else 1
        return n, [[slots[n].index((kind, first + h)) for kind in kinds] for h in range(heads)]

    near, far = lat[0]
    rel = jnp.arange(XS, dtype=jnp.int32)
    flip = jnp.arange(2, dtype=jnp.int32)
    first_rows = HEAD * 2
    owners = jnp.stack([near[:, :, 0, 2, :images], far[:, :, 0, 2, :images]]).astype(jnp.int32)
    sender = (
        ((z ^ flip) * 8)[None, :, None] + (((x + rel) & 3) * 2)[None, None, :] + (core ^ flip)[:, None, None]
    )
    block = z * 8 + ((x + rel) & 3) * 2 + core
    code = sender[..., None, None] * 4 + jnp.arange(4, dtype=jnp.int32)
    code = jnp.broadcast_to(code, owners.shape + (4,)).reshape(-1)
    owners = jnp.broadcast_to(owners[..., None], owners.shape + (4,)).reshape(-1)
    code = jnp.where(owners[None, :] == block[:, None], code[None, :], -2)
    sources = near[0, :, 0, :2].reshape(XS, first_rows).astype(jnp.int32)
    hot = (sources[:, :, None] == code[:, None, :]).astype(jnp.bfloat16)
    keep = jnp.broadcast_to((sources < 0)[:, :, None], sources.shape + (HEAD,)).astype(jnp.bfloat16)

    row_begin = (outer * 16 + z * 8 - BLOCKS) * ROWS
    ends = jnp.cumsum(doc_lengths)
    heads_of = ends - doc_lengths
    pos = (block[:, None] + outer * 16) * ROWS + jnp.arange(ROWS, dtype=jnp.int32)[None, :]
    begins = jnp.max(jnp.where(heads_of[None, None, :] <= pos[:, :, None], heads_of[None, None, :], 0), axis=2)
    begins = begins - row_begin
    mine = (block & 7) + BLOCKS
    clear = jnp.minimum((begins[:, -1] + ROWS - 1) // ROWS, mine)
    reach = jnp.stack([begins[:, 0] // ROWS, clear], axis=1).astype(jnp.int32)
    begins = begins[:, None, :].astype(jnp.int32)

    packed = pack(place, (keys, values), CHUNKS[:1]) + pack(place, (keys, values), CHUNKS[1:])
    packed_q = pack(place, (queries,), ((0, GROUP),))[0]

    kv = [across_x(parts) for parts in packed]
    q = across_x(packed_q)

    def merged(parts, chunk, kinds):
        n, own_slots = slot_of(*chunk, kinds)
        return merge(parts, *lat[n], hot, keep, chunk[1], kinds, own_slots)

    own_kv = [merged(parts, chunk, (1, 2)) for parts, chunk in zip(kv, CHUNKS)]
    query = merged(q, (0, GROUP), (0,))
    outs = []
    for own, chunk in zip(own_kv, CHUNKS):
        twin = send(own, TO_CORE)
        own_before = send(own, TO_NEXT)
        twin_before = send(own_before, TO_CORE)
        done = attend(place, reach, begins, query, own, twin, own_before, twin_before, chunk)
        outs.extend(across_x(done))
    return unpack(place, outs, CHUNKS)


def solution(mesh):
    return jax.shard_map(
        per_device,
        mesh=mesh,
        in_specs=(
            P(("outer", "inner"), None),
            P(("outer", "inner"), None),
            P(("outer", "inner"), None),
            P(("outer", "inner"), None, None),
            P(("outer", "inner")),
            P(("outer", "inner")),
            P(),
        ),
        out_specs=P(("outer", "inner"), None),
        check_vma=False,
    )
```

```python
import functools

import jax
import jax.numpy as jnp
from jax import lax
from jax.experimental import pallas as pl
from jax.experimental.pallas import tpu as pltpu
from jax.sharding import PartitionSpec as P

HEADS = 20
HEAD = 128
ROWS = 256
XS = 4
GROUP = HEADS // XS
WIDTH = GROUP * HEAD
BLOCKS = 8
LATENTS = 32
AXES = ("outer", "inner")
CHUNKS = ((0, 2), (2, 2), (4, 1))
UNROLL = 4
SLOTS = 4 + 4 * BLOCKS + 2 * UNROLL

SCALE = HEAD ** (-0.5) * 1.4426950408889634
HIDDEN = -1e30
HALVES = (slice(0, HEAD), slice(HEAD, ROWS))
MIB = 1024 * 1024
SLAB = (ROWS, HEAD)


def routes(target):
    return [(d, target(d)) for d in range(128) if 0 <= target(d) < 128]


def along_x(steps):
    return routes(lambda d: (d & ~7) | ((d + 2 * steps) & 7))


TO_CORE = routes(lambda d: d ^ 1)
TO_Z = routes(lambda d: d ^ 8)
TO_NEXT = routes(lambda d: d + 8)


def send(value, route):
    return lax.ppermute(value, AXES, route)


def across_x(parts):
    return [parts[0]] + [send(parts[XS - rel], along_x(XS - rel)) for rel in range(1, XS)]


def params(mib):
    return pltpu.CompilerParams(vmem_limit_bytes=mib * MIB)


ANY = pl.BlockSpec(memory_space=pl.ANY)
HBM = pl.BlockSpec(memory_space=pltpu.HBM)
SMEM = pl.BlockSpec(memory_space=pltpu.SMEM)
VMEM = pl.BlockSpec(memory_space=pltpu.VMEM)


def in_hbm(value):
    return pltpu.with_memory_space_constraint(value, pltpu.HBM)


def start_copies(copies, sems, first=0):
    started = [pltpu.make_async_copy(a, b, sems.at[first + n]) for n, (a, b) in enumerate(copies)]
    for copy in started:
        copy.start()
    return started


def wait_for(copies):
    for copy in copies:
        copy.wait()


def pack_kernel(parcels, small, order, place, owner, *refs):
    count = len(order)
    tensors = dict(zip(order, refs[:count]))
    refs = refs[count:]
    outs, sems = refs[: len(parcels) * XS], refs[-1]
    refs = refs[len(parcels) * XS : -1]
    copies, later = [], []
    for rel in range(XS):
        column = ((place[0] + rel) & 3) * WIDTH

        def cut(head):
            return pl.ds(pl.multiple_of(column + head * HEAD, HEAD), HEAD)

        if small:
            for s, (kind, head) in enumerate(small):
                copies.append((tensors["latents"].at[kind, :, cut(head)], refs[rel].at[2 + s]))
            later.append((refs[XS], refs[rel].at[pl.ds(0, 2)]))
        for n, parcel in enumerate(parcels):
            for s, slab in enumerate(parcel):
                target = outs[n * XS + rel].at[s]
                copies.append((tensors[slab[0]].at[:, cut(slab[1])], target))
    if small:
        notes, sources, owned = refs[XS:]
        fetched = start_copies([(owner, owned), (tensors["sources"], sources)], sems)
    started = start_copies(copies, sems, 2 if small else 0)
    if small:
        wait_for(fetched)
        row = lax.broadcasted_iota(jnp.int32, (LATENTS, HEAD), 0)
        wide = jnp.where(row == 0, sources[0:1], jnp.where(row == 1, sources[1:2], 0))
        notes[0] = wide.astype(jnp.float32).astype(jnp.bfloat16)
        owners = jnp.zeros((LATENTS, HEAD), jnp.int32)
        for image in range(LATENTS // 4):
            owners = jnp.where(row // 4 == image, owned[image], owners)
        notes[1] = owners.astype(jnp.float32).astype(jnp.bfloat16)
        started += start_copies(later, sems, 2 + len(copies))
    wait_for(started)


def pack(place, owner, tensors, parcels, small=()):
    order = tuple(tensors)
    shapes = [jax.ShapeDtypeStruct((len(parcel),) + SLAB, jnp.bfloat16) for parcel in parcels for _ in range(XS)]
    count = XS * sum(len(parcel) for parcel in parcels)
    scratch = []
    if small:
        shapes += [jax.ShapeDtypeStruct((2 + len(small), LATENTS, HEAD), jnp.bfloat16)] * XS
        count += XS * (len(small) + 1) + 2
        scratch = [
            pltpu.VMEM((2, LATENTS, HEAD), jnp.bfloat16),
            pltpu.VMEM((2, HEAD), jnp.int32),
            pltpu.SMEM(owner.shape, jnp.int32),
        ]
    given = [in_hbm(tensor) for tensor in (owner, *tensors.values())]
    outs = pl.pallas_call(
        functools.partial(pack_kernel, parcels, small, order),
        out_shape=shapes,
        in_specs=[SMEM] + [HBM] * len(given),
        out_specs=[ANY] * len(shapes),
        scratch_shapes=scratch + [pltpu.SemaphoreType.DMA((count,))],
        compiler_params=params(2),
    )(place, *given)
    return [outs[n : n + XS] for n in range(0, len(outs), XS)]


def marks_kernel(place, near, near_z, far, far_z, hot, keep):
    x, core, z = place[0], place[1], place[2]
    pieces = [source[r, 1] for source in (near, near_z, far, far_z) for r in range(XS)]
    owners = jnp.concatenate(pieces, axis=0).astype(jnp.float32).T[0:1]
    lane = lax.broadcasted_iota(jnp.int32, (1, 4 * XS * LATENTS), 1)
    from_x = (x + ((lane >> 5) & 3)) & 3
    sender = ((z ^ ((lane >> 7) & 1)) * 8) + from_x * 2 + (core ^ (lane >> 8))
    code = (sender * 4 + (lane & 3)).astype(jnp.float32)
    for rel in range(XS):
        block = (z * 8 + ((x + rel) & 3) * 2 + core).astype(jnp.float32)
        sources = jnp.concatenate([near[rel, 0, 0:1], near[rel, 0, 1:2]], axis=1).astype(jnp.float32)
        sources = jnp.broadcast_to(sources, (HEAD, ROWS)).T
        wanted = jnp.where(owners == block, code, -2.0)
        for tile in range(4):
            lanes = slice(tile * HEAD, (tile + 1) * HEAD)
            hot[rel, :, lanes] = jnp.where(sources == wanted[:, lanes], 1.0, 0.0).astype(jnp.bfloat16)
        keep[rel] = jnp.where(sources < 0, 1.0, 0.0).astype(jnp.bfloat16)


def marks(place, lat):
    return pl.pallas_call(
        marks_kernel,
        out_shape=[
            jax.ShapeDtypeStruct((XS, ROWS, 4 * XS * LATENTS), jnp.bfloat16),
            jax.ShapeDtypeStruct((XS,) + SLAB, jnp.bfloat16),
        ],
        in_specs=[SMEM] + [VMEM] * 4,
        out_specs=[VMEM] * 2,
        compiler_params=params(8),
    )(place, *lat)


def merge_kernel(base, work, *refs):
    parts, lats, (hot, keep, out, raw, lat, sems) = refs[:XS], refs[XS : XS + 4], refs[XS + 4 :]
    count = len(work)
    copies = [(parts[rel].at[pl.ds(base, count)], raw.at[rel]) for rel in range(XS)]
    started = start_copies([(lats[n], lat.at[n]) for n in range(4)] + copies, sems)
    wait_for(started)
    for n in range(0, count, 2):
        pair = work[n : n + 2]
        columns = [
            jnp.concatenate([lat[g, r, slot] for g in range(4) for r in range(XS)], axis=0) for _, slot in pair
        ]
        columns = jnp.concatenate(columns, axis=1)
        for rel in range(XS):
            kept = keep[rel] > 0
            placed = jnp.dot(hot[rel], columns, preferred_element_type=jnp.float32)
            for p, (kind, _) in enumerate(pair):
                mixed = placed[:, p * HEAD : (p + 1) * HEAD]
                mixed = jnp.where(kept, raw[rel, n + p].astype(jnp.float32), mixed)
                if kind == 2:
                    mixed = jnp.concatenate([mixed[:HEAD].T, mixed[HEAD:].T], axis=0)
                out[rel, n + p] = mixed.astype(jnp.bfloat16)


def merge(parts, base, lat, hot, keep, work):
    count = len(work)
    return pl.pallas_call(
        functools.partial(merge_kernel, base, work),
        out_shape=jax.ShapeDtypeStruct((XS, count) + SLAB, jnp.bfloat16),
        in_specs=[ANY] * (XS + 4) + [VMEM] * 2,
        out_specs=VMEM,
        scratch_shapes=[
            pltpu.VMEM((XS, count) + SLAB, jnp.bfloat16),
            pltpu.VMEM((4,) + lat[0].shape, jnp.bfloat16),
            pltpu.SemaphoreType.DMA((XS + 4,)),
        ],
        compiler_params=params(10),
    )(*parts, *lat, hot, keep)


def plan_kernel(place, lengths, begins, items):
    x, core, z, outer = place[0], place[1], place[2], place[3]
    origin = (outer * 16 + z * 8 - BLOCKS) * ROWS
    mine = [BLOCKS + 2 * ((x + rel) & 3) + core for rel in range(XS)]
    column = lax.broadcasted_iota(jnp.int32, (8, ROWS), 1)
    zero = jnp.zeros((8, ROWS), jnp.int32) - origin

    def document(d, carry):
        start, firsts, lasts, vectors = carry
        at = start - origin
        firsts = [jnp.where(at <= mine[r] * ROWS, at, firsts[r]) for r in range(XS)]
        lasts = [jnp.where(at <= mine[r] * ROWS + ROWS - 1, at, lasts[r]) for r in range(XS)]
        vectors = [jnp.where(at <= mine[r] * ROWS + column, at, vectors[r]) for r in range(XS)]
        return start + lengths[d], firsts, lasts, vectors

    least = [-origin] * XS
    _, firsts, lasts, vectors = lax.fori_loop(
        0, lengths.shape[0], document, (jnp.int32(0), least, least, [zero] * XS)
    )
    for rel in range(XS):
        begins[rel] = vectors[rel][0:1]

    def held(j):
        return jnp.where(j < BLOCKS, 8, 0) + ((j & 1) ^ core) * 4 + (((j >> 1) - x) & 3)

    def listed(count, low, high):
        for rel in range(XS):

            def add(j, count, rel=rel):
                items[0, count] = rel
                items[1, count] = j
                items[2, count] = held(j)
                return count + 1

            count = lax.fori_loop(low[rel], high[rel], add, count)
        for extra in range(UNROLL - 1):
            items[0, count + extra] = XS
            items[1, count + extra] = BLOCKS
            items[2, count + extra] = 0
        return (count + UNROLL - 1) // UNROLL * UNROLL

    for rel in range(XS):
        items[0, rel] = rel
        items[1, rel] = mine[rel]
        items[2, rel] = rel
    low = [first // ROWS for first in firsts]
    clear = [jnp.minimum((last + ROWS - 1) // ROWS, mine[rel]) for rel, last in enumerate(lasts)]
    edge = listed(XS, low, clear)
    items[3, 0] = edge
    items[3, 1] = listed(edge, clear, mine)


def plan(place, lengths):
    return pl.pallas_call(
        plan_kernel,
        out_shape=[
            jax.ShapeDtypeStruct((XS, 1, ROWS), jnp.int32),
            jax.ShapeDtypeStruct((4, SLOTS + UNROLL), jnp.int32),
        ],
        in_specs=[SMEM, SMEM],
        out_specs=[VMEM, SMEM],
        compiler_params=params(2),
    )(place, lengths)


def attend_kernel(first, heads, items, begins, q_hbm, own, twin, own_before, twin_before, *refs):
    outs, (q_buf, kv_buf, scores, best, total, accum, sems) = refs[:XS], refs[XS:]
    copies = [(q_hbm.at[:, pl.ds(first, heads)], q_buf)]
    copies += [(source, kv_buf.at[n]) for n, source in enumerate((own, twin, own_before, twin_before))]
    wait_for(start_copies(copies, sems))
    edge, end = items[3, 0], items[3, 1]

    key_row = lax.broadcasted_iota(jnp.int32, (ROWS, ROWS), 0)
    query_column = lax.broadcasted_iota(jnp.int32, (ROWS, ROWS), 1)

    for h in range(heads):
        best[...] = jnp.full(best.shape, HIDDEN, jnp.float32)
        total[...] = jnp.zeros(total.shape, jnp.float32)
        accum[...] = jnp.zeros(accum.shape, jnp.float32)

        def score(slot, edge, diagonal):
            q, j, at = items[0, slot], items[1, slot], items[2, slot]
            tile = lax.dot_general(
                kv_buf[at >> 2, at & 3, 2 * h], q_buf[q & 3, h], (((1,), (1,)), ((), ())), preferred_element_type=jnp.float32
            )
            if edge:
                seen = key_row >= begins[q & 3] - j * ROWS
                if diagonal:
                    seen = seen & (key_row <= query_column)
                tile = jnp.where(seen, tile, HIDDEN)
            scores[slot] = tile
            best[q] = jnp.maximum(best[q], jnp.max(tile.reshape(ROWS // 8, 8, ROWS), axis=0))

        def weigh(slot):
            q, at = items[0, slot], items[2, slot]
            weights = jnp.exp2(scores[slot] * SCALE - best[q, 0:1])
            total[q] = total[q] + jnp.sum(weights.reshape(ROWS // 8, 8, ROWS), axis=0)
            value = jnp.concatenate([kv_buf[at >> 2, at & 3, 2 * h + 1, half] for half in HALVES], axis=1)
            accum[q] = accum[q] + jnp.dot(value, weights.astype(jnp.bfloat16), preferred_element_type=jnp.float32)

        def grouped(low, high, one):
            def several(n, carry):
                for extra in range(UNROLL):
                    one(n * UNROLL + extra)
                return carry

            lax.fori_loop(low // UNROLL, high // UNROLL, several, 0)

        for rel in range(XS):
            score(rel, True, True)
        grouped(XS, edge, lambda slot: score(slot, True, False))
        grouped(edge, end, lambda slot: score(slot, False, False))
        for q in range(XS + 1):
            best[q] = jnp.broadcast_to(jnp.max(best[q], axis=0, keepdims=True) * SCALE, (8, ROWS))
        grouped(0, end, weigh)
        for rel in range(XS):
            mixed = accum[rel] / jnp.sum(total[rel], axis=0, keepdims=True)
            outs[rel][h] = mixed.T.astype(jnp.bfloat16)


def attend(planned, query, own, twin, own_before, twin_before, chunk):
    first, heads = chunk
    begins, items = planned
    blocks = [own, twin, own_before, twin_before]
    return pl.pallas_call(
        functools.partial(attend_kernel, first, heads),
        out_shape=[jax.ShapeDtypeStruct((heads,) + SLAB, jnp.bfloat16)] * XS,
        in_specs=[SMEM, VMEM] + [ANY] * 5,
        out_specs=[VMEM] * XS,
        scratch_shapes=[
            pltpu.VMEM((XS, heads) + SLAB, jnp.bfloat16),
            pltpu.VMEM((4, XS, 2 * heads) + SLAB, jnp.bfloat16),
            pltpu.VMEM((SLOTS, ROWS, ROWS), jnp.float32),
            pltpu.VMEM((XS + 1, 8, ROWS), jnp.float32),
            pltpu.VMEM((XS + 1, 8, ROWS), jnp.float32),
            pltpu.VMEM((XS + 1, HEAD, ROWS), jnp.float32),
            pltpu.SemaphoreType.DMA((5,)),
        ],
        compiler_params=params(16 + 3 * heads),
    )(items, begins, query, *blocks)


def unpack_kernel(chunks, place, *refs):
    parts, out, sems = refs[: len(chunks) * XS], refs[-2], refs[-1]
    copies = []
    for n, (first, heads) in enumerate(chunks):
        for rel in range(XS):
            for h in range(heads):
                begin = pl.multiple_of(((place[0] + rel) & 3) * WIDTH + (first + h) * HEAD, HEAD)
                copies.append((parts[n * XS + rel].at[h], out.at[:, pl.ds(begin, HEAD)]))
    wait_for(start_copies(copies, sems))


def unpack(place, parts, chunks, before=()):
    return pl.pallas_call(
        functools.partial(unpack_kernel, chunks),
        out_shape=jax.ShapeDtypeStruct((ROWS, HEADS * HEAD), jnp.bfloat16),
        in_specs=[SMEM] + [ANY] * len(parts) + [HBM] * len(before),
        out_specs=HBM,
        scratch_shapes=[pltpu.SemaphoreType.DMA((XS * sum(heads for _, heads in chunks),))],
        input_output_aliases={1 + len(parts): 0} if before else {},
        compiler_params=params(2),
    )(place, *parts, *before)


def joined(*values):
    return lax.optimization_barrier(values)


def per_device(queries, keys, values, latents, latent_owner, token_source, doc_lengths):
    outer = lax.axis_index("outer").astype(jnp.int32)
    inner = lax.axis_index("inner").astype(jnp.int32)
    z, x, core = inner >> 3, (inner >> 1) & 3, inner & 1
    place = jnp.stack([x, core, z, outer])
    kinds = latents.transpose(1, 0, 2)

    small = [(kind, h) for h in range(GROUP) for kind in (1, 2, 0)]
    keyed = [[(t, first + h) for h in range(heads) for t in ("k", "v")] for first, heads in CHUNKS]
    asked = [("q", h) for h in range(GROUP)]

    tensors = {"k": keys, "v": values, "latents": kinds, "sources": token_source.reshape(2, HEAD)}
    kv1, lat = pack(place, latent_owner, tensors, [keyed[0]], small)
    planned = plan(place, doc_lengths)
    lat = across_x(lat)
    lat[1], kv1 = joined(lat[1], kv1)

    near = jnp.stack(lat)
    near_z, far, kv1 = send(near, TO_Z), send(near, TO_CORE), across_x(kv1)
    cut = CHUNKS[0][1]
    second, third = keyed[1] + asked[:cut], keyed[2] + asked[cut:]
    kv2, kv3 = pack(place, latent_owner, {"k": keys, "v": values, "q": queries}, [second, third])
    near_z, far, kv1, kv2, kv3, planned = joined(near_z, far, kv1, kv2, kv3, planned)

    lat = near, near_z, far, send(near_z, TO_CORE)
    kv2 = across_x(kv2)
    hot, keep = marks(place, lat)
    kind = {"q": 0, "k": 1, "v": 2}

    def merged(parts, base, slabs):
        return merge(parts, base, lat, hot, keep, [(kind[t], 2 + small.index((kind[t], h))) for t, h in slabs])

    own1 = merged(kv1, 0, keyed[0])
    before1 = send(own1, TO_NEXT)
    twin1 = send(own1, TO_CORE)
    kv2, twin1, kv3 = joined(kv2, twin1, kv3)

    own2 = merged(kv2, 0, keyed[1])
    query1 = merged(kv2, len(keyed[1]), asked[:cut])
    before1, own2, query1, kv3 = joined(before1, own2, query1, kv3)

    before2 = send(own2, TO_NEXT)
    twin_before1 = send(before1, TO_CORE)
    kv3 = across_x(kv3)
    done1 = attend(planned, query1, own1, twin1, before1, twin_before1, (0, cut))
    kv3, done1, own2 = joined(kv3, done1, own2)

    own3 = merged(kv3, 0, keyed[2])
    query2 = merged(kv3, len(keyed[2]), asked[cut:])
    twin2 = send(own2, TO_CORE)
    out1 = across_x(done1)
    before2, own3, query2, twin2, out1 = joined(before2, own3, query2, twin2, out1)

    before3 = send(own3, TO_NEXT)
    twin_before2 = send(before2, TO_CORE)
    twin3 = send(own3, TO_CORE)
    done2 = attend(planned, query2, own2, twin2, before2, twin_before2, (0, CHUNKS[1][1]))
    out2 = across_x(done2)
    before3, out2, twin3 = joined(before3, out2, twin3)

    twin_before3 = send(before3, TO_CORE)
    done3 = attend(planned, query2, own3, twin3, before3, twin_before3, (CHUNKS[1][1], CHUNKS[2][1]))
    out3 = across_x(done3)
    mixed = unpack(place, out1 + out2, CHUNKS[:2])
    return unpack(place, out3, CHUNKS[2:], (mixed,))


def solution(mesh):
    return jax.shard_map(
        per_device,
        mesh=mesh,
        in_specs=(
            P(("outer", "inner"), None),
            P(("outer", "inner"), None),
            P(("outer", "inner"), None),
            P(("outer", "inner"), None, None),
            P(("outer", "inner")),
            P(("outer", "inner")),
            P(),
        ),
        out_specs=P(("outer", "inner"), None),
        check_vma=False,
    )
```

```python
import functools

import jax
import jax.numpy as jnp
from jax import lax
from jax.experimental import pallas as pl
from jax.experimental.pallas import tpu as pltpu
from jax.sharding import PartitionSpec as P

HEADS = 20
HEAD = 128
ROWS = 256
XS = 4
GROUP = HEADS // XS
WIDTH = GROUP * HEAD
BLOCKS = 8
LATENTS = 32
AXES = ("outer", "inner")
CHUNKS = ((0, 3), (3, 2))
UNROLL = 4
SLOTS = XS * (BLOCKS + 1) + 3 * UNROLL

SCALE = HEAD ** (-0.5) * 1.4426950408889634
HIDDEN = -1e30
HALVES = (slice(0, HEAD), slice(HEAD, ROWS))
MIB = 1024 * 1024
SLAB = (ROWS, HEAD)


def routes(target):
    return [(d, target(d)) for d in range(128) if 0 <= target(d) < 128]


def along_x(steps):
    return routes(lambda d: (d & ~7) | ((d + 2 * steps) & 7))


TO_CORE = routes(lambda d: d ^ 1)
TO_Z = routes(lambda d: d ^ 8)
TO_NEXT = routes(lambda d: d + 8)


def send(value, route):
    return lax.ppermute(value, AXES, route)


def across_x(parts):
    return [parts[0]] + [send(parts[XS - rel], along_x(XS - rel)) for rel in range(1, XS)]


def params(mib):
    return pltpu.CompilerParams(vmem_limit_bytes=mib * MIB)


ANY = pl.BlockSpec(memory_space=pl.ANY)
HBM = pl.BlockSpec(memory_space=pltpu.HBM)
SMEM = pl.BlockSpec(memory_space=pltpu.SMEM)
VMEM = pl.BlockSpec(memory_space=pltpu.VMEM)


def in_hbm(value):
    return pltpu.with_memory_space_constraint(value, pltpu.HBM)


def start_copies(copies, sems, first=0):
    started = [pltpu.make_async_copy(a, b, sems.at[first + n]) for n, (a, b) in enumerate(copies)]
    for copy in started:
        copy.start()
    return started


def wait_for(copies):
    for copy in copies:
        copy.wait()


def pack_kernel(parcels, small, order, place, owner, *refs):
    count = len(order)
    tensors = dict(zip(order, refs[:count]))
    refs = refs[count:]
    outs, sems = refs[: len(parcels) * XS], refs[-1]
    refs = refs[len(parcels) * XS : -1]
    copies, later = [], []
    for rel in range(XS):
        column = ((place[0] + rel) & 3) * WIDTH

        def cut(head):
            return pl.ds(pl.multiple_of(column + head * HEAD, HEAD), HEAD)

        if small:
            for s, (kind, head) in enumerate(small):
                copies.append((tensors["latents"].at[kind, :, cut(head)], refs[rel].at[2 + s]))
            later.append((refs[XS], refs[rel].at[pl.ds(0, 2)]))
        for n, parcel in enumerate(parcels):
            for s, slab in enumerate(parcel):
                target = outs[n * XS + rel].at[s]
                copies.append((tensors[slab[0]].at[:, cut(slab[1])], target))
    if small:
        notes, sources, owned = refs[XS:]
        fetched = start_copies([(owner, owned), (tensors["sources"], sources)], sems)
    started = start_copies(copies, sems, 2 if small else 0)
    if small:
        wait_for(fetched)
        row = lax.broadcasted_iota(jnp.int32, (LATENTS, HEAD), 0)
        wide = jnp.where(row == 0, sources[0:1], jnp.where(row == 1, sources[1:2], 0))
        notes[0] = wide.astype(jnp.float32).astype(jnp.bfloat16)
        owners = jnp.zeros((LATENTS, HEAD), jnp.int32)
        for image in range(LATENTS // 4):
            owners = jnp.where(row // 4 == image, owned[image], owners)
        notes[1] = owners.astype(jnp.float32).astype(jnp.bfloat16)
        started += start_copies(later, sems, 2 + len(copies))
    wait_for(started)


def pack(place, owner, tensors, parcels, small=()):
    order = tuple(tensors)
    shapes = [jax.ShapeDtypeStruct((len(parcel),) + SLAB, jnp.bfloat16) for parcel in parcels for _ in range(XS)]
    count = XS * sum(len(parcel) for parcel in parcels)
    scratch = []
    if small:
        shapes += [jax.ShapeDtypeStruct((2 + len(small), LATENTS, HEAD), jnp.bfloat16)] * XS
        count += XS * (len(small) + 1) + 2
        scratch = [
            pltpu.VMEM((2, LATENTS, HEAD), jnp.bfloat16),
            pltpu.VMEM((2, HEAD), jnp.int32),
            pltpu.SMEM(owner.shape, jnp.int32),
        ]
    given = [in_hbm(tensor) for tensor in (owner, *tensors.values())]
    outs = pl.pallas_call(
        functools.partial(pack_kernel, parcels, small, order),
        out_shape=shapes,
        in_specs=[SMEM] + [HBM] * len(given),
        out_specs=[ANY] * len(shapes),
        scratch_shapes=scratch + [pltpu.SemaphoreType.DMA((count,))],
        compiler_params=params(2),
    )(place, *given)
    return [outs[n : n + XS] for n in range(0, len(outs), XS)]


def marks_kernel(place, near, near_z, far, far_z, hot, keep):
    x, core, z = place[0], place[1], place[2]
    pieces = [source[r, 1] for source in (near, near_z, far, far_z) for r in range(XS)]
    owners = jnp.concatenate(pieces, axis=0).astype(jnp.float32).T[0:1]
    lane = lax.broadcasted_iota(jnp.int32, (1, 4 * XS * LATENTS), 1)
    from_x = (x + ((lane >> 5) & 3)) & 3
    sender = ((z ^ ((lane >> 7) & 1)) * 8) + from_x * 2 + (core ^ (lane >> 8))
    code = (sender * 4 + (lane & 3)).astype(jnp.float32)
    for rel in range(XS):
        block = (z * 8 + ((x + rel) & 3) * 2 + core).astype(jnp.float32)
        sources = jnp.concatenate([near[rel, 0, 0:1], near[rel, 0, 1:2]], axis=1).astype(jnp.float32)
        sources = jnp.broadcast_to(sources, (HEAD, ROWS)).T
        wanted = jnp.where(owners == block, code, -2.0)
        for tile in range(4):
            lanes = slice(tile * HEAD, (tile + 1) * HEAD)
            hot[rel, :, lanes] = jnp.where(sources == wanted[:, lanes], 1.0, 0.0).astype(jnp.bfloat16)
        keep[rel] = jnp.where(sources < 0, 1.0, 0.0).astype(jnp.bfloat16)


def marks(place, lat):
    return pl.pallas_call(
        marks_kernel,
        out_shape=[
            jax.ShapeDtypeStruct((XS, ROWS, 4 * XS * LATENTS), jnp.bfloat16),
            jax.ShapeDtypeStruct((XS,) + SLAB, jnp.bfloat16),
        ],
        in_specs=[SMEM] + [VMEM] * 4,
        out_specs=[VMEM] * 2,
        compiler_params=params(8),
    )(place, *lat)


def merge_kernel(base, work, *refs):
    parts, lats, (hot, keep, out, raw, lat, sems) = refs[:XS], refs[XS : XS + 4], refs[XS + 4 :]
    count = len(work)
    copies = [(parts[rel].at[pl.ds(base, count)], raw.at[rel]) for rel in range(XS)]
    started = start_copies([(lats[n], lat.at[n]) for n in range(4)] + copies, sems)
    wait_for(started)
    for n in range(0, count, 2):
        pair = work[n : n + 2]
        columns = [
            jnp.concatenate([lat[g, r, slot] for g in range(4) for r in range(XS)], axis=0) for _, slot in pair
        ]
        columns = jnp.concatenate(columns, axis=1)
        for rel in range(XS):
            kept = keep[rel] > 0
            placed = jnp.dot(hot[rel], columns, preferred_element_type=jnp.float32)
            for p, (kind, _) in enumerate(pair):
                mixed = placed[:, p * HEAD : (p + 1) * HEAD]
                mixed = jnp.where(kept, raw[rel, n + p].astype(jnp.float32), mixed)
                if kind == 2:
                    mixed = jnp.concatenate([mixed[:HEAD].T, mixed[HEAD:].T], axis=0)
                out[rel, n + p] = mixed.astype(jnp.bfloat16)


def merge(parts, base, lat, hot, keep, work):
    count = len(work)
    return pl.pallas_call(
        functools.partial(merge_kernel, base, work),
        out_shape=jax.ShapeDtypeStruct((XS, count) + SLAB, jnp.bfloat16),
        in_specs=[ANY] * (XS + 4) + [VMEM] * 2,
        out_specs=VMEM,
        scratch_shapes=[
            pltpu.VMEM((XS, count) + SLAB, jnp.bfloat16),
            pltpu.VMEM((4,) + lat[0].shape, jnp.bfloat16),
            pltpu.SemaphoreType.DMA((XS + 4,)),
        ],
        compiler_params=params(10),
    )(*parts, *lat, hot, keep)


def plan_kernel(place, lengths, begins, items):
    x, core, z, outer = place[0], place[1], place[2], place[3]
    origin = (outer * 16 + z * 8 - BLOCKS) * ROWS
    mine = [BLOCKS + 2 * ((x + rel) & 3) + core for rel in range(XS)]
    column = lax.broadcasted_iota(jnp.int32, (8, ROWS), 1)
    zero = jnp.zeros((8, ROWS), jnp.int32) - origin

    def document(d, carry):
        start, firsts, lasts, vectors = carry
        at = start - origin
        firsts = [jnp.where(at <= mine[r] * ROWS, at, firsts[r]) for r in range(XS)]
        lasts = [jnp.where(at <= mine[r] * ROWS + ROWS - 1, at, lasts[r]) for r in range(XS)]
        vectors = [jnp.where(at <= mine[r] * ROWS + column, at, vectors[r]) for r in range(XS)]
        return start + lengths[d], firsts, lasts, vectors

    least = [-origin] * XS
    _, firsts, lasts, vectors = lax.fori_loop(
        0, lengths.shape[0], document, (jnp.int32(0), least, least, [zero] * XS)
    )
    for rel in range(XS):
        begins[rel] = vectors[rel][0:1]

    def held(j):
        return jnp.where(j < BLOCKS, 8, 0) + ((j & 1) ^ core) * 4 + (((j >> 1) - x) & 3)

    def listed(count, low, high):
        for rel in range(XS):

            def add(j, count, rel=rel):
                items[0, count] = rel
                items[1, count] = j
                items[2, count] = held(j)
                return count + 1

            count = lax.fori_loop(low[rel], high[rel], add, count)
        for extra in range(UNROLL - 1):
            items[0, count + extra] = XS
            items[1, count + extra] = BLOCKS
            items[2, count + extra] = spare
        return (count + UNROLL - 1) // UNROLL * UNROLL

    for rel in range(XS):
        items[0, rel] = rel
        items[1, rel] = mine[rel]
        items[2, rel] = rel
    low = [first // ROWS for first in firsts]
    clear = [jnp.clip((last + ROWS - 1) // ROWS, BLOCKS, mine[rel]) for rel, last in enumerate(lasts)]
    spare = 0
    edge = listed(XS, [jnp.maximum(at, BLOCKS) for at in low], clear)
    end = listed(edge, clear, mine)
    spare = 2 * XS
    items[3, 0] = edge
    items[3, 1] = end
    items[3, 2] = listed(end, low, [BLOCKS] * XS)


def plan(place, lengths):
    return pl.pallas_call(
        plan_kernel,
        out_shape=[
            jax.ShapeDtypeStruct((XS, 1, ROWS), jnp.int32),
            jax.ShapeDtypeStruct((4, SLOTS + UNROLL), jnp.int32),
        ],
        in_specs=[SMEM, SMEM],
        out_specs=[VMEM, SMEM],
        compiler_params=params(2),
    )(place, lengths)


def attend_kernel(part, query_at, slab_at, state_at, heads, items, begins, q_hbm, *refs):
    sources = 4 if part == "all" else 2
    lowest = 2 if part == "before" else 0
    kept, refs = refs[:sources], refs[sources:]
    if part == "before":
        state, refs = refs[:3], refs[3:]
    count = 3 if part == "own" else XS
    outs, (q_buf, kv_buf, scores, best, total, accum, sems) = refs[:count], refs[count:]
    copies = [(q_hbm.at[:, pl.ds(query_at, heads)], q_buf)]
    copies += [(source.at[:, pl.ds(slab_at, 2 * heads)], kv_buf.at[n]) for n, source in enumerate(kept)]
    wait_for(start_copies(copies, sems))
    edge, end, last = items[3, 0], items[3, 1], items[3, 2]
    begin = end if part == "before" else 0
    stop = end if part == "own" else last

    key_row = lax.broadcasted_iota(jnp.int32, (ROWS, ROWS), 0)
    query_column = lax.broadcasted_iota(jnp.int32, (ROWS, ROWS), 1)

    for h in range(heads):
        best[...] = jnp.full(best.shape, HIDDEN, jnp.float32)
        total[...] = jnp.zeros(total.shape, jnp.float32)
        accum[...] = jnp.zeros(accum.shape, jnp.float32)
        if part == "before":
            for q in range(XS):
                best[q] = state[0][state_at + h, q]

        def score(slot, masked, diagonal):
            q, j, at = items[0, slot], items[1, slot], items[2, slot] - lowest * XS
            tile = lax.dot_general(
                kv_buf[at >> 2, at & 3, 2 * h],
                q_buf[q & 3, h],
                (((1,), (1,)), ((), ())),
                preferred_element_type=jnp.float32,
            )
            if masked:
                seen = key_row >= begins[q & 3] - j * ROWS
                if diagonal:
                    seen = seen & (key_row <= query_column)
                tile = jnp.where(seen, tile, HIDDEN)
            scores[slot] = tile
            best[q] = jnp.maximum(best[q], jnp.max(tile.reshape(ROWS // 8, 8, ROWS), axis=0))

        def weigh(slot):
            q, at = items[0, slot], items[2, slot] - lowest * XS
            weights = jnp.exp2(scores[slot] * SCALE - best[q, 0:1])
            total[q] = total[q] + jnp.sum(weights.reshape(ROWS // 8, 8, ROWS), axis=0)
            value = jnp.concatenate([kv_buf[at >> 2, at & 3, 2 * h + 1, half] for half in HALVES], axis=1)
            accum[q] = accum[q] + jnp.dot(value, weights.astype(jnp.bfloat16), preferred_element_type=jnp.float32)

        def grouped(low, high, one):
            def several(n, carry):
                for extra in range(UNROLL):
                    one(low + n * UNROLL + extra)
                return carry

            lax.fori_loop(0, (high - low) // UNROLL, several, 0)

        if part != "before":
            for rel in range(XS):
                score(rel, True, True)
            grouped(XS, edge, lambda slot: score(slot, True, False))
            grouped(edge, end, lambda slot: score(slot, False, False))
        if part != "own":
            grouped(end, last, lambda slot: score(slot, True, False))
        for q in range(XS + 1):
            top = jnp.max(best[q], axis=0, keepdims=True)
            if part == "before" and q < XS:
                shrink = jnp.exp2((state[0][state_at + h, q, 0:1] - top) * SCALE)
                total[q] = state[1][state_at + h, q] * shrink
                accum[q] = state[2][state_at + h, q] * shrink
            if part == "own" and q < XS:
                outs[0][h, q] = jnp.broadcast_to(top, (8, ROWS))
            best[q] = jnp.broadcast_to(top * SCALE, (8, ROWS))
        grouped(begin, stop, weigh)
        for rel in range(XS):
            if part == "own":
                outs[1][h, rel] = total[rel]
                outs[2][h, rel] = accum[rel]
            else:
                mixed = accum[rel] / jnp.sum(total[rel], axis=0, keepdims=True)
                outs[rel][h] = mixed.T.astype(jnp.bfloat16)


def attend(part, planned, query, sources, heads, query_at=0, head_at=0, state=()):
    begins, items = planned
    if part == "own":
        shapes = [(heads, XS, 8, ROWS), (heads, XS, 8, ROWS), (heads, XS, HEAD, ROWS)]
        shapes = [jax.ShapeDtypeStruct(shape, jnp.float32) for shape in shapes]
    else:
        shapes = [jax.ShapeDtypeStruct((heads,) + SLAB, jnp.bfloat16)] * XS
    return pl.pallas_call(
        functools.partial(attend_kernel, part, query_at, 2 * head_at, head_at, heads),
        out_shape=shapes,
        in_specs=[SMEM, VMEM] + [ANY] * (1 + len(sources)) + [VMEM] * len(state),
        out_specs=[VMEM] * len(shapes),
        scratch_shapes=[
            pltpu.VMEM((XS, heads) + SLAB, jnp.bfloat16),
            pltpu.VMEM((len(sources), XS, 2 * heads) + SLAB, jnp.bfloat16),
            pltpu.VMEM((SLOTS, ROWS, ROWS), jnp.float32),
            pltpu.VMEM((XS + 1, 8, ROWS), jnp.float32),
            pltpu.VMEM((XS + 1, 8, ROWS), jnp.float32),
            pltpu.VMEM((XS + 1, HEAD, ROWS), jnp.float32),
            pltpu.SemaphoreType.DMA((5,)),
        ],
        compiler_params=params(24 + 2 * heads),
    )(items, begins, query, *sources, *state)


def unpack_kernel(chunks, place, *refs):
    parts, out, sems = refs[: len(chunks) * XS], refs[-2], refs[-1]
    copies = []
    for n, (first, heads) in enumerate(chunks):
        for rel in range(XS):
            for h in range(heads):
                begin = pl.multiple_of(((place[0] + rel) & 3) * WIDTH + (first + h) * HEAD, HEAD)
                copies.append((parts[n * XS + rel].at[h], out.at[:, pl.ds(begin, HEAD)]))
    wait_for(start_copies(copies, sems))


def unpack(place, parts, chunks, before=()):
    return pl.pallas_call(
        functools.partial(unpack_kernel, chunks),
        out_shape=jax.ShapeDtypeStruct((ROWS, HEADS * HEAD), jnp.bfloat16),
        in_specs=[SMEM] + [ANY] * len(parts) + [HBM] * len(before),
        out_specs=HBM,
        scratch_shapes=[pltpu.SemaphoreType.DMA((XS * sum(heads for _, heads in chunks),))],
        input_output_aliases={1 + len(parts): 0} if before else {},
        compiler_params=params(2),
    )(place, *parts, *before)


def joined(*values):
    return lax.optimization_barrier(values)


def per_device(queries, keys, values, latents, latent_owner, token_source, doc_lengths):
    outer = lax.axis_index("outer").astype(jnp.int32)
    inner = lax.axis_index("inner").astype(jnp.int32)
    z, x, core = inner >> 3, (inner >> 1) & 3, inner & 1
    place = jnp.stack([x, core, z, outer])
    kinds = latents.transpose(1, 0, 2)

    small = [(kind, h) for h in range(GROUP) for kind in (1, 2, 0)]
    keyed = [[(t, first + h) for h in range(heads) for t in ("k", "v")] for first, heads in CHUNKS]
    asked = [("q", h) for h in range(GROUP)]

    tensors = {"k": keys, "v": values, "latents": kinds, "sources": token_source.reshape(2, HEAD)}
    kv1, lat = pack(place, latent_owner, tensors, [keyed[0]], small)
    planned = plan(place, doc_lengths)
    lat = across_x(lat)
    lat[1], kv1 = joined(lat[1], kv1)

    near = jnp.stack(lat)
    near_z, far, kv1 = send(near, TO_Z), send(near, TO_CORE), across_x(kv1)
    (kv2,) = pack(place, latent_owner, {"k": keys, "v": values, "q": queries}, [keyed[1] + asked])
    near_z, far, kv1, kv2, planned = joined(near_z, far, kv1, kv2, planned)

    lat = near, near_z, far, send(near_z, TO_CORE)
    kv2 = across_x(kv2)
    hot, keep = marks(place, lat)
    kind = {"q": 0, "k": 1, "v": 2}

    def merged(parts, base, slabs):
        return merge(parts, base, lat, hot, keep, [(kind[t], 2 + small.index((kind[t], h))) for t, h in slabs])

    own1 = merged(kv1, 0, keyed[0])
    before1 = send(own1, TO_NEXT)
    twin1 = send(own1, TO_CORE)
    kv2, twin1 = joined(kv2, twin1)

    own2 = merged(kv2, 0, keyed[1])
    query = merged(kv2, len(keyed[1]), asked)
    before1, own1, own2, query = joined(before1, own1, own2, query)

    before2 = send(own2, TO_NEXT)
    first, second = CHUNKS[0][1], CHUNKS[1][1]
    sources = before1, send(before1, TO_CORE)
    state = attend("own", planned, query, (own1, twin1), first)
    done1 = attend("before", planned, query, sources, first, 0, 0, state)
    twin2 = send(own2, TO_CORE)
    out1 = across_x(done1)
    state = attend("own", planned, query, (own2, twin2), second, first)
    before2, out1[1], out1[3], state = joined(before2, out1[1], out1[3], state)

    sources = before2, send(before2, TO_CORE)
    out2 = across_x(attend("before", planned, query, sources, second, first, 0, state))
    mixed = unpack(place, out1, CHUNKS[:1])
    return unpack(place, out2, CHUNKS[1:], (mixed,))


def solution(mesh):
    return jax.shard_map(
        per_device,
        mesh=mesh,
        in_specs=(
            P(("outer", "inner"), None),
            P(("outer", "inner"), None),
            P(("outer", "inner"), None),
            P(("outer", "inner"), None, None),
            P(("outer", "inner")),
            P(("outer", "inner")),
            P(),
        ),
        out_specs=P(("outer", "inner"), None),
        check_vma=False,
    )
```

```python
import functools

import jax
import jax.numpy as jnp
from jax import lax
from jax.experimental import pallas as pl
from jax.experimental.pallas import tpu as pltpu
from jax.sharding import PartitionSpec as P

HEADS = 20
HEAD = 128
ROWS = 256
XS = 4
GROUP = HEADS // XS
WIDTH = GROUP * HEAD
BLOCKS = 8
LATENTS = 32
AXES = ("outer", "inner")
CHUNKS = ((0, 3), (3, 2))
UNROLL = 4
SLOTS = XS * (BLOCKS + 1) + 3 * UNROLL

SCALE = HEAD ** (-0.5) * 1.4426950408889634
HIDDEN = -1e30
HALVES = (slice(0, HEAD), slice(HEAD, ROWS))
MIB = 1024 * 1024
SLAB = (ROWS, HEAD)


def routes(target):
    return [(d, target(d)) for d in range(128) if 0 <= target(d) < 128]


def along_x(steps):
    return routes(lambda d: (d & ~7) | ((d + 2 * steps) & 7))


TO_CORE = routes(lambda d: d ^ 1)
TO_Z = routes(lambda d: d ^ 8)
TO_NEXT = routes(lambda d: d + 8)


def send(value, route):
    return lax.ppermute(value, AXES, route)


def across_x(parts):
    return [parts[0]] + [send(parts[XS - rel], along_x(XS - rel)) for rel in range(1, XS)]


def params(mib):
    return pltpu.CompilerParams(vmem_limit_bytes=mib * MIB)


ANY = pl.BlockSpec(memory_space=pl.ANY)
HBM = pl.BlockSpec(memory_space=pltpu.HBM)
SMEM = pl.BlockSpec(memory_space=pltpu.SMEM)
VMEM = pl.BlockSpec(memory_space=pltpu.VMEM)


def in_hbm(value):
    return pltpu.with_memory_space_constraint(value, pltpu.HBM)


def start_copies(copies, sems, first=0):
    started = [pltpu.make_async_copy(a, b, sems.at[first + n]) for n, (a, b) in enumerate(copies)]
    for copy in started:
        copy.start()
    return started


def wait_for(copies):
    for copy in copies:
        copy.wait()


def pack_kernel(parcels, small, order, place, owner, *refs):
    count = len(order)
    tensors = dict(zip(order, refs[:count]))
    refs = refs[count:]
    outs, sems = refs[: len(parcels) * XS], refs[-1]
    refs = refs[len(parcels) * XS : -1]
    copies, later = [], []
    for rel in range(XS):
        column = ((place[0] + rel) & 3) * WIDTH

        def cut(head):
            return pl.ds(pl.multiple_of(column + head * HEAD, HEAD), HEAD)

        if small:
            for s, (kind, head) in enumerate(small):
                copies.append((tensors["latents"].at[kind, :, cut(head)], refs[rel].at[2 + s]))
            later.append((refs[XS], refs[rel].at[pl.ds(0, 2)]))
        for n, parcel in enumerate(parcels):
            for s, slab in enumerate(parcel):
                target = outs[n * XS + rel].at[s]
                copies.append((tensors[slab[0]].at[:, cut(slab[1])], target))
    if small:
        notes, sources, owned = refs[XS:]
        fetched = start_copies([(owner, owned), (tensors["sources"], sources)], sems)
    started = start_copies(copies, sems, 2 if small else 0)
    if small:
        wait_for(fetched)
        row = lax.broadcasted_iota(jnp.int32, (LATENTS, HEAD), 0)
        wide = jnp.where(row == 0, sources[0:1], jnp.where(row == 1, sources[1:2], 0))
        notes[0] = wide.astype(jnp.float32).astype(jnp.bfloat16)
        owners = jnp.zeros((LATENTS, HEAD), jnp.int32)
        for image in range(LATENTS // 4):
            owners = jnp.where(row // 4 == image, owned[image], owners)
        notes[1] = owners.astype(jnp.float32).astype(jnp.bfloat16)
        started += start_copies(later, sems, 2 + len(copies))
    wait_for(started)


def pack(place, owner, tensors, parcels, small=()):
    order = tuple(tensors)
    shapes = [jax.ShapeDtypeStruct((len(parcel),) + SLAB, jnp.bfloat16) for parcel in parcels for _ in range(XS)]
    count = XS * sum(len(parcel) for parcel in parcels)
    scratch = []
    if small:
        shapes += [jax.ShapeDtypeStruct((2 + len(small), LATENTS, HEAD), jnp.bfloat16)] * XS
        count += XS * (len(small) + 1) + 2
        scratch = [
            pltpu.VMEM((2, LATENTS, HEAD), jnp.bfloat16),
            pltpu.VMEM((2, HEAD), jnp.int32),
            pltpu.SMEM(owner.shape, jnp.int32),
        ]
    given = [in_hbm(tensor) for tensor in (owner, *tensors.values())]
    outs = pl.pallas_call(
        functools.partial(pack_kernel, parcels, small, order),
        out_shape=shapes,
        in_specs=[SMEM] + [HBM] * len(given),
        out_specs=[ANY] * len(shapes),
        scratch_shapes=scratch + [pltpu.SemaphoreType.DMA((count,))],
        compiler_params=params(2),
    )(place, *given)
    return [outs[n : n + XS] for n in range(0, len(outs), XS)]


def marks_kernel(place, near, near_z, far, far_z, hot, keep):
    x, core, z = place[0], place[1], place[2]
    pieces = [source[r, 1] for source in (near, near_z, far, far_z) for r in range(XS)]
    owners = jnp.concatenate(pieces, axis=0).astype(jnp.float32).T[0:1]
    lane = lax.broadcasted_iota(jnp.int32, (1, 4 * XS * LATENTS), 1)
    from_x = (x + ((lane >> 5) & 3)) & 3
    sender = ((z ^ ((lane >> 7) & 1)) * 8) + from_x * 2 + (core ^ (lane >> 8))
    code = (sender * 4 + (lane & 3)).astype(jnp.float32)
    for rel in range(XS):
        block = (z * 8 + ((x + rel) & 3) * 2 + core).astype(jnp.float32)
        sources = jnp.concatenate([near[rel, 0, 0:1], near[rel, 0, 1:2]], axis=1).astype(jnp.float32)
        sources = jnp.broadcast_to(sources, (HEAD, ROWS)).T
        wanted = jnp.where(owners == block, code, -2.0)
        for tile in range(4):
            lanes = slice(tile * HEAD, (tile + 1) * HEAD)
            hot[rel, :, lanes] = jnp.where(sources == wanted[:, lanes], 1.0, 0.0).astype(jnp.bfloat16)
        keep[rel] = jnp.where(sources < 0, 1.0, 0.0).astype(jnp.bfloat16)


def marks(place, lat):
    return pl.pallas_call(
        marks_kernel,
        out_shape=[
            jax.ShapeDtypeStruct((XS, ROWS, 4 * XS * LATENTS), jnp.bfloat16),
            jax.ShapeDtypeStruct((XS,) + SLAB, jnp.bfloat16),
        ],
        in_specs=[SMEM] + [VMEM] * 4,
        out_specs=[VMEM] * 2,
        compiler_params=params(8),
    )(place, *lat)


def merge_kernel(base, work, *refs):
    parts, lats, (hot, keep, out, raw, lat, sems) = refs[:XS], refs[XS : XS + 4], refs[XS + 4 :]
    count = len(work)
    copies = [(parts[rel].at[pl.ds(base, count)], raw.at[rel]) for rel in range(XS)]
    started = start_copies([(lats[n], lat.at[n]) for n in range(4)] + copies, sems)
    wait_for(started)
    for n in range(0, count, 2):
        pair = work[n : n + 2]
        columns = [
            jnp.concatenate([lat[g, r, slot] for g in range(4) for r in range(XS)], axis=0) for _, slot in pair
        ]
        columns = jnp.concatenate(columns, axis=1)
        for rel in range(XS):
            kept = keep[rel] > 0
            placed = jnp.dot(hot[rel], columns, preferred_element_type=jnp.float32)
            for p, (kind, _) in enumerate(pair):
                mixed = placed[:, p * HEAD : (p + 1) * HEAD]
                mixed = jnp.where(kept, raw[rel, n + p].astype(jnp.float32), mixed)
                if kind == 2:
                    mixed = jnp.concatenate([mixed[:HEAD].T, mixed[HEAD:].T], axis=0)
                out[rel, n + p] = mixed.astype(jnp.bfloat16)


def merge(parts, base, lat, hot, keep, work):
    count = len(work)
    return pl.pallas_call(
        functools.partial(merge_kernel, base, work),
        out_shape=jax.ShapeDtypeStruct((XS, count) + SLAB, jnp.bfloat16),
        in_specs=[ANY] * (XS + 4) + [VMEM] * 2,
        out_specs=VMEM,
        scratch_shapes=[
            pltpu.VMEM((XS, count) + SLAB, jnp.bfloat16),
            pltpu.VMEM((4,) + lat[0].shape, jnp.bfloat16),
            pltpu.SemaphoreType.DMA((XS + 4,)),
        ],
        compiler_params=params(10),
    )(*parts, *lat, hot, keep)


def plan_kernel(place, lengths, begins, items):
    x, core, z, outer = place[0], place[1], place[2], place[3]
    origin = (outer * 16 + z * 8 - BLOCKS) * ROWS
    mine = [BLOCKS + 2 * ((x + rel) & 3) + core for rel in range(XS)]
    column = lax.broadcasted_iota(jnp.int32, (8, ROWS), 1)
    zero = jnp.zeros((8, ROWS), jnp.int32) - origin

    def document(d, carry):
        start, firsts, lasts, vectors = carry
        at = start - origin
        firsts = [jnp.where(at <= mine[r] * ROWS, at, firsts[r]) for r in range(XS)]
        lasts = [jnp.where(at <= mine[r] * ROWS + ROWS - 1, at, lasts[r]) for r in range(XS)]
        vectors = [jnp.where(at <= mine[r] * ROWS + column, at, vectors[r]) for r in range(XS)]
        return start + lengths[d], firsts, lasts, vectors

    least = [-origin] * XS
    _, firsts, lasts, vectors = lax.fori_loop(
        0, lengths.shape[0], document, (jnp.int32(0), least, least, [zero] * XS)
    )
    for rel in range(XS):
        begins[rel] = vectors[rel][0:1]

    def held(j):
        return jnp.where(j < BLOCKS, 8, 0) + ((j & 1) ^ core) * 4 + (((j >> 1) - x) & 3)

    def listed(count, low, high):
        for rel in range(XS):

            def add(j, count, rel=rel):
                items[0, count] = rel
                items[1, count] = j
                items[2, count] = held(j)
                return count + 1

            count = lax.fori_loop(low[rel], high[rel], add, count)
        for extra in range(UNROLL - 1):
            items[0, count + extra] = XS
            items[1, count + extra] = BLOCKS
            items[2, count + extra] = spare
        return (count + UNROLL - 1) // UNROLL * UNROLL

    for rel in range(XS):
        items[0, rel] = rel
        items[1, rel] = mine[rel]
        items[2, rel] = rel
    low = [first // ROWS for first in firsts]
    clear = [jnp.clip((last + ROWS - 1) // ROWS, BLOCKS, mine[rel]) for rel, last in enumerate(lasts)]
    spare = 0
    edge = listed(XS, [jnp.maximum(at, BLOCKS) for at in low], clear)
    end = listed(edge, clear, mine)
    spare = 2 * XS
    items[3, 0] = edge
    items[3, 1] = end
    items[3, 2] = listed(end, low, [BLOCKS] * XS)


def plan(place, lengths):
    return pl.pallas_call(
        plan_kernel,
        out_shape=[
            jax.ShapeDtypeStruct((XS, 1, ROWS), jnp.int32),
            jax.ShapeDtypeStruct((4, SLOTS + UNROLL), jnp.int32),
        ],
        in_specs=[SMEM, SMEM],
        out_specs=[VMEM, SMEM],
        compiler_params=params(2),
    )(place, lengths)


def attend_kernel(part, query_at, slab_at, state_at, heads, items, begins, q_hbm, *refs):
    sources = 4 if part == "all" else 2
    lowest = 2 if part == "before" else 0
    kept, refs = refs[:sources], refs[sources:]
    if part == "before":
        state, refs = refs[:3], refs[3:]
    count = 3 if part == "own" else XS
    outs, (q_buf, kv_buf, scores, best, total, accum, sems) = refs[:count], refs[count:]
    copies = [(q_hbm.at[:, pl.ds(query_at, heads)], q_buf)]
    copies += [(source.at[:, pl.ds(slab_at, 2 * heads)], kv_buf.at[n]) for n, source in enumerate(kept)]
    wait_for(start_copies(copies, sems))
    edge, end, last = items[3, 0], items[3, 1], items[3, 2]
    begin = end if part == "before" else 0
    stop = end if part == "own" else last

    key_row = lax.broadcasted_iota(jnp.int32, (ROWS, ROWS), 0)
    query_column = lax.broadcasted_iota(jnp.int32, (ROWS, ROWS), 1)

    for h in range(heads):
        best[...] = jnp.full(best.shape, HIDDEN, jnp.float32)
        total[...] = jnp.zeros(total.shape, jnp.float32)
        accum[...] = jnp.zeros(accum.shape, jnp.float32)
        if part == "before":
            for q in range(XS):
                best[q] = state[0][state_at + h, q]

        def score(slot, masked, diagonal):
            q, j, at = items[0, slot], items[1, slot], items[2, slot] - lowest * XS
            tile = lax.dot_general(
                kv_buf[at >> 2, at & 3, 2 * h],
                q_buf[q & 3, h],
                (((1,), (1,)), ((), ())),
                preferred_element_type=jnp.float32,
            )
            if masked:
                seen = key_row >= begins[q & 3] - j * ROWS
                if diagonal:
                    seen = seen & (key_row <= query_column)
                tile = jnp.where(seen, tile, HIDDEN)
            scores[slot] = tile
            best[q] = jnp.maximum(best[q], jnp.max(tile.reshape(ROWS // 8, 8, ROWS), axis=0))

        def weigh(slot):
            q, at = items[0, slot], items[2, slot] - lowest * XS
            weights = jnp.exp2(scores[slot] * SCALE - best[q, 0:1])
            total[q] = total[q] + jnp.sum(weights.reshape(ROWS // 8, 8, ROWS), axis=0)
            value = jnp.concatenate([kv_buf[at >> 2, at & 3, 2 * h + 1, half] for half in HALVES], axis=1)
            accum[q] = accum[q] + jnp.dot(value, weights.astype(jnp.bfloat16), preferred_element_type=jnp.float32)

        def grouped(low, high, one):
            def several(n, carry):
                for extra in range(UNROLL):
                    one(low + n * UNROLL + extra)
                return carry

            lax.fori_loop(0, (high - low) // UNROLL, several, 0)

        if part != "before":
            for rel in range(XS):
                score(rel, True, True)
            grouped(XS, edge, lambda slot: score(slot, True, False))
            grouped(edge, end, lambda slot: score(slot, False, False))
        if part != "own":
            grouped(end, last, lambda slot: score(slot, True, False))
        for q in range(XS + 1):
            top = jnp.max(best[q], axis=0, keepdims=True)
            if part == "before" and q < XS:
                shrink = jnp.exp2((state[0][state_at + h, q, 0:1] - top) * SCALE)
                total[q] = state[1][state_at + h, q] * shrink
                accum[q] = state[2][state_at + h, q] * shrink
            if part == "own" and q < XS:
                outs[0][h, q] = jnp.broadcast_to(top, (8, ROWS))
            best[q] = jnp.broadcast_to(top * SCALE, (8, ROWS))
        grouped(begin, stop, weigh)
        for rel in range(XS):
            if part == "own":
                outs[1][h, rel] = total[rel]
                outs[2][h, rel] = accum[rel]
            else:
                mixed = accum[rel] / jnp.sum(total[rel], axis=0, keepdims=True)
                outs[rel][h] = mixed.T.astype(jnp.bfloat16)


def attend(part, planned, query, sources, heads, query_at=0, head_at=0, state=()):
    begins, items = planned
    if part == "own":
        shapes = [(heads, XS, 8, ROWS), (heads, XS, 8, ROWS), (heads, XS, HEAD, ROWS)]
        shapes = [jax.ShapeDtypeStruct(shape, jnp.float32) for shape in shapes]
    else:
        shapes = [jax.ShapeDtypeStruct((heads,) + SLAB, jnp.bfloat16)] * XS
    return pl.pallas_call(
        functools.partial(attend_kernel, part, query_at, 2 * head_at, head_at, heads),
        out_shape=shapes,
        in_specs=[SMEM, VMEM] + [ANY] * (1 + len(sources)) + [VMEM] * len(state),
        out_specs=[VMEM] * len(shapes),
        scratch_shapes=[
            pltpu.VMEM((XS, heads) + SLAB, jnp.bfloat16),
            pltpu.VMEM((len(sources), XS, 2 * heads) + SLAB, jnp.bfloat16),
            pltpu.VMEM((SLOTS, ROWS, ROWS), jnp.float32),
            pltpu.VMEM((XS + 1, 8, ROWS), jnp.float32),
            pltpu.VMEM((XS + 1, 8, ROWS), jnp.float32),
            pltpu.VMEM((XS + 1, HEAD, ROWS), jnp.float32),
            pltpu.SemaphoreType.DMA((5,)),
        ],
        compiler_params=params(24 + 2 * heads),
    )(items, begins, query, *sources, *state)


def unpack_kernel(chunks, place, *refs):
    parts, out, sems = refs[: len(chunks) * XS], refs[-2], refs[-1]
    copies = []
    for n, (first, heads) in enumerate(chunks):
        for rel in range(XS):
            for h in range(heads):
                begin = pl.multiple_of(((place[0] + rel) & 3) * WIDTH + (first + h) * HEAD, HEAD)
                copies.append((parts[n * XS + rel].at[h], out.at[:, pl.ds(begin, HEAD)]))
    wait_for(start_copies(copies, sems))


def unpack(place, parts, chunks, before=()):
    return pl.pallas_call(
        functools.partial(unpack_kernel, chunks),
        out_shape=jax.ShapeDtypeStruct((ROWS, HEADS * HEAD), jnp.bfloat16),
        in_specs=[SMEM] + [ANY] * len(parts) + [HBM] * len(before),
        out_specs=HBM,
        scratch_shapes=[pltpu.SemaphoreType.DMA((XS * sum(heads for _, heads in chunks),))],
        input_output_aliases={1 + len(parts): 0} if before else {},
        compiler_params=params(2),
    )(place, *parts, *before)


def joined(*values):
    return lax.optimization_barrier(values)


def per_device(queries, keys, values, latents, latent_owner, token_source, doc_lengths):
    outer = lax.axis_index("outer").astype(jnp.int32)
    inner = lax.axis_index("inner").astype(jnp.int32)
    z, x, core = inner >> 3, (inner >> 1) & 3, inner & 1
    place = jnp.stack([x, core, z, outer])
    kinds = latents.transpose(1, 0, 2)

    small = [(kind, h) for h in range(GROUP) for kind in (1, 2, 0)]
    keyed = [[(t, first + h) for h in range(heads) for t in ("k", "v")] for first, heads in CHUNKS]
    asked = [("q", h) for h in range(GROUP)]

    tensors = {"k": keys, "v": values, "latents": kinds, "sources": token_source.reshape(2, HEAD)}
    kv1, lat = pack(place, latent_owner, tensors, [keyed[0]], small)
    planned = plan(place, doc_lengths)
    lat = across_x(lat)
    lat[1], kv1 = joined(lat[1], kv1)

    near = jnp.stack(lat)
    near_z, far, kv1 = send(near, TO_Z), send(near, TO_CORE), across_x(kv1)
    kv2, q = pack(place, latent_owner, {"k": keys, "v": values, "q": queries}, [keyed[1], asked])
    near_z, far, kv1, kv2, q, planned = joined(near_z, far, kv1, kv2, q, planned)

    lat = near, near_z, far, send(near_z, TO_CORE)
    q = across_x(q)
    hot, keep = marks(place, lat)
    kind = {"q": 0, "k": 1, "v": 2}

    def merged(parts, slabs):
        return merge(parts, 0, lat, hot, keep, [(kind[t], 2 + small.index((kind[t], h))) for t, h in slabs])

    own1 = merged(kv1, keyed[0])
    before1 = send(own1, TO_NEXT)
    twin1 = send(own1, TO_CORE)
    q, twin1, kv2 = joined(q, twin1, kv2)

    kv2 = across_x(kv2)
    query = merged(q, asked)
    first, second = CHUNKS[0][1], CHUNKS[1][1]
    state = attend("own", planned, query, (own1, twin1), first)
    own2 = merged(kv2, keyed[1])
    before1, own2, state = joined(before1, own2, state)

    before2 = send(own2, TO_NEXT)
    sources = before1, send(before1, TO_CORE)
    done1 = attend("before", planned, query, sources, first, 0, 0, state)
    twin2 = send(own2, TO_CORE)
    out1 = across_x(done1)
    state = attend("own", planned, query, (own2, twin2), second, first)
    mixed = unpack(place, out1, CHUNKS[:1])
    before2, mixed, state = joined(before2, mixed, state)

    sources = before2, send(before2, TO_CORE)
    out2 = across_x(attend("before", planned, query, sources, second, first, 0, state))
    return unpack(place, out2, CHUNKS[1:], (mixed,))


def solution(mesh):
    return jax.shard_map(
        per_device,
        mesh=mesh,
        in_specs=(
            P(("outer", "inner"), None),
            P(("outer", "inner"), None),
            P(("outer", "inner"), None),
            P(("outer", "inner"), None, None),
            P(("outer", "inner")),
            P(("outer", "inner")),
            P(),
        ),
        out_specs=P(("outer", "inner"), None),
        check_vma=False,
    )
```

```python
import functools

import jax
import jax.numpy as jnp
from jax import lax
from jax.experimental import pallas as pl
from jax.experimental.pallas import tpu as pltpu
from jax.sharding import PartitionSpec as P

HEADS = 20
HEAD = 128
ROWS = 256
XS = 4
GROUP = HEADS // XS
WIDTH = GROUP * HEAD
BLOCKS = 8
LATENTS = 32
AXES = ("outer", "inner")
CHUNKS = ((0, 3), (3, 2))
UNROLL = 4
SLOTS = XS * (BLOCKS + 1) + 3 * UNROLL

SCALE = HEAD ** (-0.5) * 1.4426950408889634
HIDDEN = -1e30
HALVES = (slice(0, HEAD), slice(HEAD, ROWS))
MIB = 1024 * 1024
SLAB = (ROWS, HEAD)


def routes(target):
    return [(d, target(d)) for d in range(128) if 0 <= target(d) < 128]


def along_x(steps):
    return routes(lambda d: (d & ~7) | ((d + 2 * steps) & 7))


TO_CORE = routes(lambda d: d ^ 1)
TO_Z = routes(lambda d: d ^ 8)
TO_NEXT = routes(lambda d: d + 8)


def send(value, route):
    return lax.ppermute(value, AXES, route)


def across_x(parts):
    return [parts[0]] + [send(parts[XS - rel], along_x(XS - rel)) for rel in range(1, XS)]


def params(mib):
    return pltpu.CompilerParams(vmem_limit_bytes=mib * MIB)


ANY = pl.BlockSpec(memory_space=pl.ANY)
HBM = pl.BlockSpec(memory_space=pltpu.HBM)
SMEM = pl.BlockSpec(memory_space=pltpu.SMEM)
VMEM = pl.BlockSpec(memory_space=pltpu.VMEM)


def in_hbm(value):
    return pltpu.with_memory_space_constraint(value, pltpu.HBM)


def start_copies(copies, sems, first=0):
    started = [pltpu.make_async_copy(a, b, sems.at[first + n]) for n, (a, b) in enumerate(copies)]
    for copy in started:
        copy.start()
    return started


def wait_for(copies):
    for copy in copies:
        copy.wait()


def pack_kernel(parcels, small, order, place, owner, *refs):
    count = len(order)
    tensors = dict(zip(order, refs[:count]))
    refs = refs[count:]
    outs, sems = refs[: len(parcels) * XS], refs[-1]
    refs = refs[len(parcels) * XS : -1]
    copies, later = [], []
    for rel in range(XS):
        column = ((place[0] + rel) & 3) * WIDTH

        def cut(head):
            return pl.ds(pl.multiple_of(column + head * HEAD, HEAD), HEAD)

        if small:
            for s, (kind, head) in enumerate(small):
                copies.append((tensors["latents"].at[kind, :, cut(head)], refs[rel].at[2 + s]))
            later.append((refs[XS], refs[rel].at[pl.ds(0, 2)]))
        for n, parcel in enumerate(parcels):
            for s, slab in enumerate(parcel):
                target = outs[n * XS + rel].at[s]
                copies.append((tensors[slab[0]].at[:, cut(slab[1])], target))
    if small:
        notes, sources, owned = refs[XS:]
        fetched = start_copies([(owner, owned), (tensors["sources"], sources)], sems)
    started = start_copies(copies, sems, 2 if small else 0)
    if small:
        wait_for(fetched)
        row = lax.broadcasted_iota(jnp.int32, (LATENTS, HEAD), 0)
        wide = jnp.where(row == 0, sources[0:1], jnp.where(row == 1, sources[1:2], 0))
        notes[0] = wide.astype(jnp.float32).astype(jnp.bfloat16)
        owners = jnp.zeros((LATENTS, HEAD), jnp.int32)
        for image in range(LATENTS // 4):
            owners = jnp.where(row // 4 == image, owned[image], owners)
        notes[1] = owners.astype(jnp.float32).astype(jnp.bfloat16)
        started += start_copies(later, sems, 2 + len(copies))
    wait_for(started)


def pack(place, owner, tensors, parcels, small=()):
    order = tuple(tensors)
    shapes = [jax.ShapeDtypeStruct((len(parcel),) + SLAB, jnp.bfloat16) for parcel in parcels for _ in range(XS)]
    count = XS * sum(len(parcel) for parcel in parcels)
    scratch = []
    if small:
        shapes += [jax.ShapeDtypeStruct((2 + len(small), LATENTS, HEAD), jnp.bfloat16)] * XS
        count += XS * (len(small) + 1) + 2
        scratch = [
            pltpu.VMEM((2, LATENTS, HEAD), jnp.bfloat16),
            pltpu.VMEM((2, HEAD), jnp.int32),
            pltpu.SMEM(owner.shape, jnp.int32),
        ]
    given = [in_hbm(tensor) for tensor in (owner, *tensors.values())]
    outs = pl.pallas_call(
        functools.partial(pack_kernel, parcels, small, order),
        out_shape=shapes,
        in_specs=[SMEM] + [HBM] * len(given),
        out_specs=[ANY] * len(shapes),
        scratch_shapes=scratch + [pltpu.SemaphoreType.DMA((count,))],
        compiler_params=params(2),
    )(place, *given)
    return [outs[n : n + XS] for n in range(0, len(outs), XS)]


def marks_kernel(place, near, near_z, far, far_z, hot, keep):
    x, core, z = place[0], place[1], place[2]
    pieces = [source[r, 1] for source in (near, near_z, far, far_z) for r in range(XS)]
    owners = jnp.concatenate(pieces, axis=0).astype(jnp.float32).T[0:1]
    lane = lax.broadcasted_iota(jnp.int32, (1, 4 * XS * LATENTS), 1)
    from_x = (x + ((lane >> 5) & 3)) & 3
    sender = ((z ^ ((lane >> 7) & 1)) * 8) + from_x * 2 + (core ^ (lane >> 8))
    code = (sender * 4 + (lane & 3)).astype(jnp.float32)
    for rel in range(XS):
        block = (z * 8 + ((x + rel) & 3) * 2 + core).astype(jnp.float32)
        sources = jnp.concatenate([near[rel, 0, 0:1], near[rel, 0, 1:2]], axis=1).astype(jnp.float32)
        sources = jnp.broadcast_to(sources, (HEAD, ROWS)).T
        wanted = jnp.where(owners == block, code, -2.0)
        for tile in range(4):
            lanes = slice(tile * HEAD, (tile + 1) * HEAD)
            hot[rel, :, lanes] = jnp.where(sources == wanted[:, lanes], 1.0, 0.0).astype(jnp.bfloat16)
        keep[rel] = jnp.where(sources < 0, 1.0, 0.0).astype(jnp.bfloat16)


def marks(place, lat):
    return pl.pallas_call(
        marks_kernel,
        out_shape=[
            jax.ShapeDtypeStruct((XS, ROWS, 4 * XS * LATENTS), jnp.bfloat16),
            jax.ShapeDtypeStruct((XS,) + SLAB, jnp.bfloat16),
        ],
        in_specs=[SMEM] + [VMEM] * 4,
        out_specs=[VMEM] * 2,
        compiler_params=params(8),
    )(place, *lat)


def merge_kernel(base, work, *refs):
    parts, lats, (hot, keep, out, raw, lat, sems) = refs[:XS], refs[XS : XS + 4], refs[XS + 4 :]
    count = len(work)
    copies = [(parts[rel].at[pl.ds(base, count)], raw.at[rel]) for rel in range(XS)]
    started = start_copies([(lats[n], lat.at[n]) for n in range(4)] + copies, sems)
    wait_for(started)
    for n in range(0, count, 2):
        pair = work[n : n + 2]
        columns = [
            jnp.concatenate([lat[g, r, slot] for g in range(4) for r in range(XS)], axis=0) for _, slot in pair
        ]
        columns = jnp.concatenate(columns, axis=1)
        for rel in range(XS):
            kept = keep[rel] > 0
            placed = jnp.dot(hot[rel], columns, preferred_element_type=jnp.float32)
            for p, (kind, _) in enumerate(pair):
                mixed = placed[:, p * HEAD : (p + 1) * HEAD]
                mixed = jnp.where(kept, raw[rel, n + p].astype(jnp.float32), mixed)
                if kind == 2:
                    mixed = jnp.concatenate([mixed[:HEAD].T, mixed[HEAD:].T], axis=0)
                out[rel, n + p] = mixed.astype(jnp.bfloat16)


def merge(parts, base, lat, hot, keep, work):
    count = len(work)
    return pl.pallas_call(
        functools.partial(merge_kernel, base, work),
        out_shape=jax.ShapeDtypeStruct((XS, count) + SLAB, jnp.bfloat16),
        in_specs=[ANY] * (XS + 4) + [VMEM] * 2,
        out_specs=VMEM,
        scratch_shapes=[
            pltpu.VMEM((XS, count) + SLAB, jnp.bfloat16),
            pltpu.VMEM((4,) + lat[0].shape, jnp.bfloat16),
            pltpu.SemaphoreType.DMA((XS + 4,)),
        ],
        compiler_params=params(10),
    )(*parts, *lat, hot, keep)


def plan_kernel(place, lengths, begins, items):
    x, core, z, outer = place[0], place[1], place[2], place[3]
    origin = (outer * 16 + z * 8 - BLOCKS) * ROWS
    mine = [BLOCKS + 2 * ((x + rel) & 3) + core for rel in range(XS)]
    column = lax.broadcasted_iota(jnp.int32, (8, ROWS), 1)
    zero = jnp.zeros((8, ROWS), jnp.int32) - origin

    def document(d, carry):
        start, firsts, lasts, vectors = carry
        at = start - origin
        firsts = [jnp.where(at <= mine[r] * ROWS, at, firsts[r]) for r in range(XS)]
        lasts = [jnp.where(at <= mine[r] * ROWS + ROWS - 1, at, lasts[r]) for r in range(XS)]
        vectors = [jnp.where(at <= mine[r] * ROWS + column, at, vectors[r]) for r in range(XS)]
        return start + lengths[d], firsts, lasts, vectors

    least = [-origin] * XS
    _, firsts, lasts, vectors = lax.fori_loop(
        0, lengths.shape[0], document, (jnp.int32(0), least, least, [zero] * XS)
    )
    for rel in range(XS):
        begins[rel] = vectors[rel][0:1]

    def held(j):
        return jnp.where(j < BLOCKS, 8, 0) + ((j & 1) ^ core) * 4 + (((j >> 1) - x) & 3)

    def listed(count, low, high):
        for rel in range(XS):

            def add(j, count, rel=rel):
                items[0, count] = rel
                items[1, count] = j
                items[2, count] = held(j)
                return count + 1

            count = lax.fori_loop(low[rel], high[rel], add, count)
        for extra in range(UNROLL - 1):
            items[0, count + extra] = XS
            items[1, count + extra] = BLOCKS
            items[2, count + extra] = spare
        return (count + UNROLL - 1) // UNROLL * UNROLL

    for rel in range(XS):
        items[0, rel] = rel
        items[1, rel] = mine[rel]
        items[2, rel] = rel
    low = [first // ROWS for first in firsts]
    clear = [jnp.clip((last + ROWS - 1) // ROWS, BLOCKS, mine[rel]) for rel, last in enumerate(lasts)]
    spare = 0
    edge = listed(XS, [jnp.maximum(at, BLOCKS) for at in low], clear)
    end = listed(edge, clear, mine)
    spare = 2 * XS
    items[3, 0] = edge
    items[3, 1] = end
    items[3, 2] = listed(end, low, [BLOCKS] * XS)


def plan(place, lengths):
    return pl.pallas_call(
        plan_kernel,
        out_shape=[
            jax.ShapeDtypeStruct((XS, 1, ROWS), jnp.int32),
            jax.ShapeDtypeStruct((4, SLOTS + UNROLL), jnp.int32),
        ],
        in_specs=[SMEM, SMEM],
        out_specs=[VMEM, SMEM],
        compiler_params=params(2),
    )(place, lengths)


def attend_kernel(part, query_at, slab_at, state_at, heads, items, begins, q_hbm, *refs):
    sources = 4 if part == "all" else 2
    lowest = 2 if part == "before" else 0
    kept, refs = refs[:sources], refs[sources:]
    if part == "before":
        state, refs = refs[:3], refs[3:]
    count = 3 if part == "own" else XS
    outs, (q_buf, kv_buf, scores, best, total, accum, sems) = refs[:count], refs[count:]
    copies = [(q_hbm.at[:, pl.ds(query_at, heads)], q_buf)]
    copies += [(source.at[:, pl.ds(slab_at, 2 * heads)], kv_buf.at[n]) for n, source in enumerate(kept)]
    wait_for(start_copies(copies, sems))
    edge, end, last = items[3, 0], items[3, 1], items[3, 2]
    begin = end if part == "before" else 0
    stop = end if part == "own" else last

    key_row = lax.broadcasted_iota(jnp.int32, (ROWS, ROWS), 0)
    query_column = lax.broadcasted_iota(jnp.int32, (ROWS, ROWS), 1)

    for h in range(heads):
        best[...] = jnp.full(best.shape, HIDDEN, jnp.float32)
        total[...] = jnp.zeros(total.shape, jnp.float32)
        accum[...] = jnp.zeros(accum.shape, jnp.float32)
        if part == "before":
            for q in range(XS):
                best[q] = state[0][state_at + h, q]

        def score(slot, masked, diagonal):
            q, j, at = items[0, slot], items[1, slot], items[2, slot] - lowest * XS
            tile = lax.dot_general(
                kv_buf[at >> 2, at & 3, 2 * h],
                q_buf[q & 3, h],
                (((1,), (1,)), ((), ())),
                preferred_element_type=jnp.float32,
            )
            if masked:
                seen = key_row >= begins[q & 3] - j * ROWS
                if diagonal:
                    seen = seen & (key_row <= query_column)
                tile = jnp.where(seen, tile, HIDDEN)
            scores[slot] = tile
            best[q] = jnp.maximum(best[q], jnp.max(tile.reshape(ROWS // 8, 8, ROWS), axis=0))

        def weigh(slot):
            q, at = items[0, slot], items[2, slot] - lowest * XS
            weights = jnp.exp2(scores[slot] * SCALE - best[q, 0:1])
            total[q] = total[q] + jnp.sum(weights.reshape(ROWS // 8, 8, ROWS), axis=0)
            value = jnp.concatenate([kv_buf[at >> 2, at & 3, 2 * h + 1, half] for half in HALVES], axis=1)
            accum[q] = accum[q] + jnp.dot(value, weights.astype(jnp.bfloat16), preferred_element_type=jnp.float32)

        def grouped(low, high, one):
            def several(n, carry):
                for extra in range(UNROLL):
                    one(low + n * UNROLL + extra)
                return carry

            lax.fori_loop(0, (high - low) // UNROLL, several, 0)

        if part != "before":
            for rel in range(XS):
                score(rel, True, True)
            grouped(XS, edge, lambda slot: score(slot, True, False))
            grouped(edge, end, lambda slot: score(slot, False, False))
        if part != "own":
            grouped(end, last, lambda slot: score(slot, True, False))
        for q in range(XS + 1):
            top = jnp.max(best[q], axis=0, keepdims=True)
            if part == "before" and q < XS:
                shrink = jnp.exp2((state[0][state_at + h, q, 0:1] - top) * SCALE)
                total[q] = state[1][state_at + h, q] * shrink
                accum[q] = state[2][state_at + h, q] * shrink
            if part == "own" and q < XS:
                outs[0][h, q] = jnp.broadcast_to(top, (8, ROWS))
            best[q] = jnp.broadcast_to(top * SCALE, (8, ROWS))
        grouped(begin, stop, weigh)
        for rel in range(XS):
            if part == "own":
                outs[1][h, rel] = total[rel]
                outs[2][h, rel] = accum[rel]
            else:
                mixed = accum[rel] / jnp.sum(total[rel], axis=0, keepdims=True)
                outs[rel][h] = mixed.T.astype(jnp.bfloat16)


def attend(part, planned, query, sources, heads, query_at=0, head_at=0, state=()):
    begins, items = planned
    if part == "own":
        shapes = [(heads, XS, 8, ROWS), (heads, XS, 8, ROWS), (heads, XS, HEAD, ROWS)]
        shapes = [jax.ShapeDtypeStruct(shape, jnp.float32) for shape in shapes]
    else:
        shapes = [jax.ShapeDtypeStruct((heads,) + SLAB, jnp.bfloat16)] * XS
    return pl.pallas_call(
        functools.partial(attend_kernel, part, query_at, 2 * head_at, head_at, heads),
        out_shape=shapes,
        in_specs=[SMEM, VMEM] + [ANY] * (1 + len(sources)) + [VMEM] * len(state),
        out_specs=[VMEM] * len(shapes),
        scratch_shapes=[
            pltpu.VMEM((XS, heads) + SLAB, jnp.bfloat16),
            pltpu.VMEM((len(sources), XS, 2 * heads) + SLAB, jnp.bfloat16),
            pltpu.VMEM((SLOTS, ROWS, ROWS), jnp.float32),
            pltpu.VMEM((XS + 1, 8, ROWS), jnp.float32),
            pltpu.VMEM((XS + 1, 8, ROWS), jnp.float32),
            pltpu.VMEM((XS + 1, HEAD, ROWS), jnp.float32),
            pltpu.SemaphoreType.DMA((5,)),
        ],
        compiler_params=params(24 + 2 * heads),
    )(items, begins, query, *sources, *state)


def unpack_kernel(chunks, place, *refs):
    parts, out, sems = refs[: len(chunks) * XS], refs[-2], refs[-1]
    copies = []
    for n, (first, heads) in enumerate(chunks):
        for rel in range(XS):
            for h in range(heads):
                begin = pl.multiple_of(((place[0] + rel) & 3) * WIDTH + (first + h) * HEAD, HEAD)
                copies.append((parts[n * XS + rel].at[h], out.at[:, pl.ds(begin, HEAD)]))
    wait_for(start_copies(copies, sems))


def unpack(place, parts, chunks, before=()):
    return pl.pallas_call(
        functools.partial(unpack_kernel, chunks),
        out_shape=jax.ShapeDtypeStruct((ROWS, HEADS * HEAD), jnp.bfloat16),
        in_specs=[SMEM] + [ANY] * len(parts) + [HBM] * len(before),
        out_specs=HBM,
        scratch_shapes=[pltpu.SemaphoreType.DMA((XS * sum(heads for _, heads in chunks),))],
        input_output_aliases={1 + len(parts): 0} if before else {},
        compiler_params=params(2),
    )(place, *parts, *before)


def joined(*values):
    return lax.optimization_barrier(values)


def per_device(queries, keys, values, latents, latent_owner, token_source, doc_lengths):
    outer = lax.axis_index("outer").astype(jnp.int32)
    inner = lax.axis_index("inner").astype(jnp.int32)
    z, x, core = inner >> 3, (inner >> 1) & 3, inner & 1
    place = jnp.stack([x, core, z, outer])
    kinds = latents.transpose(1, 0, 2)

    small = [(kind, h) for h in range(GROUP) for kind in (1, 2, 0)]
    keyed = [[(t, first + h) for h in range(heads) for t in ("k", "v")] for first, heads in CHUNKS]
    asked = [("q", h) for h in range(GROUP)]

    tensors = {"latents": kinds, "sources": token_source.reshape(2, HEAD)}
    (lat,) = pack(place, latent_owner, tensors, [], small)
    (kv1,) = pack(place, latent_owner, {"k": keys, "v": values}, [keyed[0]])
    planned = plan(place, doc_lengths)
    lat = across_x(lat)
    lat[1], kv1 = joined(lat[1], kv1)

    near = jnp.stack(lat)
    near_z, far, kv1 = send(near, TO_Z), send(near, TO_CORE), across_x(kv1)
    kv2, q = pack(place, latent_owner, {"k": keys, "v": values, "q": queries}, [keyed[1], asked])
    near_z, far, kv1, kv2, q, planned = joined(near_z, far, kv1, kv2, q, planned)

    lat = near, near_z, far, send(near_z, TO_CORE)
    q = across_x(q)
    hot, keep = marks(place, lat)
    kind = {"q": 0, "k": 1, "v": 2}

    def merged(parts, slabs):
        return merge(parts, 0, lat, hot, keep, [(kind[t], 2 + small.index((kind[t], h))) for t, h in slabs])

    own1 = merged(kv1, keyed[0])
    before1 = send(own1, TO_NEXT)
    twin1 = send(own1, TO_CORE)
    q, twin1, kv2 = joined(q, twin1, kv2)

    kv2 = across_x(kv2)
    query = merged(q, asked)
    first, second = CHUNKS[0][1], CHUNKS[1][1]
    state = attend("own", planned, query, (own1, twin1), first)
    own2 = merged(kv2, keyed[1])
    before1, own2, state = joined(before1, own2, state)

    before2 = send(own2, TO_NEXT)
    sources = before1, send(before1, TO_CORE)
    done1 = attend("before", planned, query, sources, first, 0, 0, state)
    twin2 = send(own2, TO_CORE)
    out1 = across_x(done1)
    state = attend("own", planned, query, (own2, twin2), second, first)
    mixed = unpack(place, out1, CHUNKS[:1])
    before2, mixed, state = joined(before2, mixed, state)

    sources = before2, send(before2, TO_CORE)
    out2 = across_x(attend("before", planned, query, sources, second, first, 0, state))
    return unpack(place, out2, CHUNKS[1:], (mixed,))


def solution(mesh):
    return jax.shard_map(
        per_device,
        mesh=mesh,
        in_specs=(
            P(("outer", "inner"), None),
            P(("outer", "inner"), None),
            P(("outer", "inner"), None),
            P(("outer", "inner"), None, None),
            P(("outer", "inner")),
            P(("outer", "inner")),
            P(),
        ),
        out_specs=P(("outer", "inner"), None),
        check_vma=False,
    )
```
